512 devices in a mesh: row: 16 (over x, z_lo), col: 32 (over y, z_hi, core).
Axes of the slice: x: 4, y: 4, z: 16 (z_hi: 4, z_lo: 4; z = z_hi * 4 + z_lo), core: 2. Of those that a mesh axis runs over, the one named last changes fastest.
Arguments:
- out_grad: bfloat16 [1024, 8192], P('col', 'row'), may hold values from -6 to 6
- layer_input: bfloat16 [1024, 8192], P('col', 'row'), may hold values from -6 to 6
- gate_preact: bfloat16 [1024, 14784], P('row', 'col'), may hold values from -8 to 8
- up_preact: bfloat16 [1024, 14784], P('row', 'col'), may hold values from -6 to 6
- w_down: bfloat16 [8192, 14784], P('row', 'col'), may hold values from -0.0625 to 0.0625
- w_gate: bfloat16 [14784, 8192], P('col', 'row'), may hold values from -0.046875 to 0.046875
- w_up: bfloat16 [14784, 8192], P('col', 'row'), may hold values from -0.046875 to 0.046875
Outputs:
- input_grad: bfloat16 [1024, 8192], P('col', 'row')
- down_grad: bfloat16 [8192, 14784], P('row', 'col')
- gate_grad: bfloat16 [14784, 8192], P('col', 'row')
- up_grad: bfloat16 [14784, 8192], P('col', 'row')
The draws below stay inside these ranges and needn't reach their ends.
All inputs are finite; a program needn't handle non-finite values.
Results may differ from the reference program's by a relative error of at most 0.005.
Values may be sent and summed in bfloat16 or wider, within the bound.
A program may use at most 64 MiB of HBM per device.

```python
import jax
import jax.numpy as jnp
from jax import lax

D = 8192
FF = 14784
TOKENS = 1024


def shard_levels(rng, dims, pieces, low, top_value):
    factor_of = 1.0
    for dim, shards_of in pieces:
        draws = jax.random.uniform(jax.random.fold_in(jax.random.fold_in(rng, 6), dim), (shards_of,), jnp.float32, low / len(pieces), top_value / len(pieces))
        factor_of = factor_of * jnp.repeat(jnp.exp(draws), dims[dim] // shards_of).reshape((-1,) + (1,) * (len(dims) - 1 - dim))
    return factor_of


def centred(own_key, dims, spread, most, pieces=(), kind=jnp.bfloat16):
    factor_of = shard_levels(own_key, dims, pieces, -0.22, 0.18) if pieces else 1.0
    result = jax.random.normal(own_key, dims, jnp.float32) * spread * factor_of
    return jnp.minimum(jnp.maximum(result, -most), most).astype(kind)


def setup_inputs(seed: int = 0) -> dict:
    splits = jax.random.split(jax.random.key(seed), 8)
    return {
        "out_grad": centred(splits[0], (TOKENS, D), 1.0, 6.0, ((0, 32), (1, 16))),
        "layer_input": centred(splits[1], (TOKENS, D), 1.0, 6.0, ((0, 32), (1, 16))),
        "gate_preact": centred(splits[2], (TOKENS, FF), 1.5, 8.0, ((0, 16), (1, 32))),
        "up_preact": centred(splits[3], (TOKENS, FF), 1.0, 6.0, ((0, 16), (1, 32))),
        "w_down": centred(splits[4], (D, FF), D ** -0.5, 0.0625, ((0, 16), (1, 32))),
        "w_gate": centred(splits[5], (FF, D), FF ** -0.5, 0.046875, ((0, 32), (1, 16))),
        "w_up": centred(splits[6], (FF, D), FF ** -0.5, 0.046875, ((0, 32), (1, 16))),
    }


def swiglu_back(back_hidden, gate_preact, up_preact):
    gate = gate_preact.astype(jnp.float32)
    upper = up_preact.astype(jnp.float32)
    sig = jax.nn.sigmoid(gate)
    gate_back = (back_hidden * upper * sig * (1.0 + gate * (1.0 - sig))).astype(jnp.bfloat16)
    upward_back = (back_hidden * gate * sig).astype(jnp.bfloat16)
    return gate_back, upward_back


def contract_tokens(left, right):
    return lax.dot_general(left, right, (((0,), (0,)), ((), ())), preferred_element_type=jnp.float32)


def reference(out_grad, layer_input, gate_preact, up_preact, w_down, w_gate, w_up):
    gate = gate_preact.astype(jnp.float32)
    hidden = (gate * jax.nn.sigmoid(gate) * up_preact.astype(jnp.float32)).astype(jnp.bfloat16)
    back_hidden = jnp.dot(out_grad, w_down, preferred_element_type=jnp.float32)
    gate_back, upward_back = swiglu_back(back_hidden, gate_preact, up_preact)
    input_sum = jnp.dot(gate_back, w_gate, preferred_element_type=jnp.float32) + jnp.dot(upward_back, w_up, preferred_element_type=jnp.float32)
    input_grad = input_sum.astype(jnp.bfloat16)
    down_grad = contract_tokens(out_grad, hidden).astype(jnp.bfloat16)
    gate_grad = contract_tokens(gate_back, layer_input).astype(jnp.bfloat16)
    up_grad = contract_tokens(upward_back, layer_input).astype(jnp.bfloat16)
    return input_grad, down_grad, gate_grad, up_grad
```

```python
import functools

import jax
import jax.numpy as jnp
from jax import lax
from jax.experimental import pallas as pl
from jax.experimental.pallas import tpu as pltpu
from jax.sharding import PartitionSpec as P

BF = jnp.bfloat16
F32 = jnp.float32
MESH = pl.DeviceIdType.MESH
N_COPIES = 128
WIDE = 512


def rounded(value):
    return value.astype(BF)


def dot(left, right, dims):
    return lax.dot_general(left, right, (dims, ((), ())), preferred_element_type=F32)


NN = ((1,), (0,))
NT = ((1,), (1,))
TN = ((0,), (0,))


def kernel(
    og_in, li_in, gp_in, up_in, wd_in, wg_in, wu_in,
    ig_out, dg_out, gg_out, ug_out,
    grads, inputs, hidden, backs,
    gp, up, wd_raw, wg_raw, wu_raw, wd, wg, wu,
    part, part_bf, far_lo, far_hi, from_lo, from_hi, z_send, z_recv,
    ipart, ipart_sib, iq, iq_bf, ifar_lo, ifar_hi, ifrom_lo, ifrom_hi, iz_send, iz_recv,
    gg_acc, ug_acc, gg, ug, dg, ig,
    local_sem, send_sem, recv_sem,
):
    units = gp_in.shape[1]
    row, col = lax.axis_index("row"), lax.axis_index("col")
    x, zl = lax.div(row, 4), lax.rem(row, 4)
    y, zh, core = lax.div(col, 8), lax.rem(lax.div(col, 2), 4), lax.rem(col, 2)
    sib = 1 - core

    def on(value, step):
        return lax.rem(value + step + 4, 4)

    xp, xm, xo = on(x, 1), on(x, -1), on(x, 2)
    yp, ym, yo = on(y, 1), on(y, -1), on(y, 2)
    hp, hm, ho = on(zh, 1), on(zh, -1), on(zh, 2)

    def row_of(a, b):
        return a * 4 + b

    def col_of(a, b, k):
        return (a * 4 + b) * 2 + k

    X_UP, X_DN = (row_of(xp, zl), col), (row_of(xm, zl), col)
    Y_UP, Y_DN = (row, col_of(yp, zh, core)), (row, col_of(ym, zh, core))
    H_UP, H_DN, H_OP = (
        (row, col_of(y, hp, core)),
        (row, col_of(y, hm, core)),
        (row, col_of(y, ho, core)),
    )
    L_TO = [(row_of(x, on(zl, d)), col) for d in (1, 2, 3)]
    SIB = (row, col_of(y, zh, sib))

    locals_ = []

    def local(src, dst):
        copy = pltpu.make_async_copy(src, dst, local_sem.at[len(locals_)])
        locals_.append(copy)
        copy.start()
        return copy

    sent = []

    def send(src, dst, where):
        k = len(sent)
        copy = pltpu.make_async_remote_copy(
            src_ref=src,
            dst_ref=dst,
            send_sem=send_sem.at[k],
            recv_sem=recv_sem.at[k],
            device_id=where,
            device_id_type=MESH,
        )
        copy.start()
        sent.append(copy)
        return copy

    own = row_of(y, zh)
    c_og = local(og_in, grads.at[own, core])
    c_gp = local(gp_in, gp)
    c_up = local(up_in, up)
    c_wd = local(wd_in, wd_raw)
    c_li = local(li_in, inputs.at[own, core])
    c_wg = local(wg_in, wg_raw)
    c_wu = local(wu_in, wu_raw)

    barrier = pltpu.get_barrier_semaphore()
    partners = [X_UP, X_DN, Y_UP, Y_DN, H_UP, H_DN, H_OP, SIB] + L_TO
    for where in partners:
        pl.semaphore_signal(barrier, inc=1, device_id=where, device_id_type=MESH)
    pl.semaphore_wait(barrier, len(partners))

    def share(block):
        ref = grads.at[row_of(y, block), core]
        return send(ref, ref, Y_UP), send(ref, ref, Y_DN), send(ref, ref, SIB)

    def here(ref, index):
        return ref.at[index, core]

    g_up = send(og_in, here(grads, own), H_UP)
    g_dn = send(og_in, here(grads, own), H_DN)
    y0 = (
        send(og_in, here(grads, own), Y_UP),
        send(og_in, here(grads, own), Y_DN),
        send(og_in, here(grads, own), SIB),
    )

    c_gp.wait()
    c_up.wait()
    gate = gp[...].astype(F32)
    upper = up[...].astype(F32)
    sig = jax.nn.sigmoid(gate)
    hidden[row] = jnp.zeros((64, WIDE), BF)
    hidden[row, :, 0:units] = rounded(gate * sig * upper)
    c_wd.wait()
    wd[...] = jnp.zeros((WIDE, wd.shape[1]), BF)
    wd[0:units, :] = wd_raw[...]

    y0[0].wait_recv()
    ref = here(grads, row_of(ym, zh))
    f_up0 = send(ref, ref, Y_UP)
    g_up.wait_recv()
    ref = grads.at[row_of(y, hm), core, pl.ds(0, 16)]
    g_up2 = send(ref, ref, H_UP)
    y1 = share(hm)
    g_dn.wait_recv()
    ref = grads.at[row_of(y, hp), core, pl.ds(16, 16)]
    g_dn2 = send(ref, ref, H_DN)
    y2 = share(hp)
    y1[1].wait_recv()
    ref = here(grads, row_of(yp, hm))
    f_dn1 = send(ref, ref, Y_DN)
    y2[0].wait_recv()
    ref = here(grads, row_of(ym, hp))
    f_up2 = send(ref, ref, Y_UP)
    g_up2.wait_recv()
    g_dn2.wait_recv()
    y3 = share(ho)

    i_up = send(li_in, here(inputs, own), H_UP)
    i_dn = send(li_in, here(inputs, own), H_DN)
    h_z = [send(hidden.at[row], hidden.at[row], where) for where in L_TO]

    def plane(ref, a):
        return ref.at[pl.ds(a * 4, 4)]

    def plane_core(ref, a, k):
        return ref.at[pl.ds(a * 4, 4), k]

    def partial(a):
        rows = grads[pl.ds(a * 4, 4)].reshape(256, grads.shape[3])
        out = dot(rows, wd[...], NT).reshape(4, 64, WIDE)
        part[pl.ds(a * 4, 4)] = out
        part_bf[pl.ds(a * 4, 4)] = rounded(out)

    y3[1].wait_recv()
    ref = here(grads, row_of(yp, ho))
    f_dn3 = send(ref, ref, Y_DN)
    c_og.wait()
    y0[2].wait_recv()
    y1[2].wait_recv()
    y2[2].wait_recv()
    y3[2].wait_recv()
    partial(y)
    y1[0].wait_recv()
    y3[0].wait_recv()
    s_ym = send(plane_core(grads, ym, core), plane_core(grads, ym, core), SIB)
    y0[1].wait_recv()
    y2[1].wait_recv()
    s_yp = send(plane_core(grads, yp, core), plane_core(grads, yp, core), SIB)
    s_ym.wait_recv()
    partial(ym)
    f_up0.wait_recv()
    f_up2.wait_recv()
    f_dn1.wait_recv()
    f_dn3.wait_recv()
    s_yo = send(plane_core(grads, yo, core), plane_core(grads, yo, core), SIB)
    s_yp.wait_recv()
    partial(yp)
    s_yo.wait_recv()
    partial(yo)

    def two(ref, a, b):
        return ref.at[pl.ds(a * 4 + b, 2)]

    r_up = send(two(part_bf, xo, 0), far_lo, X_UP)
    r_dn = send(two(part_bf, xo, 2), far_hi, X_DN)
    e_up = send(two(part_bf, xp, 2), from_lo.at[pl.ds(2, 2)], X_UP)
    e_dn = send(two(part_bf, xm, 0), from_hi.at[pl.ds(0, 2)], X_DN)

    i_up.wait_recv()
    ref = inputs.at[row_of(y, hm), core, pl.ds(0, 16)]
    i_up2 = send(ref, ref, H_UP)
    i_dn.wait_recv()
    ref = inputs.at[row_of(y, hp), core, pl.ds(16, 16)]
    i_dn2 = send(ref, ref, H_DN)

    r_up.wait_recv()
    part_bf[pl.ds(xp * 4, 2)] = rounded(part[pl.ds(xp * 4, 2)] + far_lo[...].astype(F32))
    l_up = send(two(part_bf, xp, 0), from_lo.at[pl.ds(0, 2)], X_UP)
    r_dn.wait_recv()
    part_bf[pl.ds(xm * 4 + 2, 2)] = rounded(part[pl.ds(xm * 4 + 2, 2)] + far_hi[...].astype(F32))
    l_dn = send(two(part_bf, xm, 2), from_hi.at[pl.ds(2, 2)], X_DN)

    i_up2.wait_recv()
    i_dn2.wait_recv()
    c_li.wait()
    ref = plane_core(inputs, y, core)
    iy_up, iy_dn, iy_s = send(ref, ref, Y_UP), send(ref, ref, Y_DN), send(ref, ref, SIB)

    def hidden_x(b):
        ref = hidden.at[row_of(x, b)]
        return send(ref, ref, X_UP), send(ref, ref, X_DN)

    hx = [hidden_x(zl)]
    for d in (1, 2, 3):
        h_z[d - 1].wait_recv()
        hx.append(hidden_x(on(zl, -d)))

    c_wg.wait()
    c_wu.wait()
    wg[...] = jnp.zeros((WIDE, wg.shape[1]), BF)
    wg[0:units, :] = wg_raw[...]
    wu[...] = jnp.zeros((WIDE, wu.shape[1]), BF)
    wu[0:units, :] = wu_raw[...]

    e_up.wait_recv()
    e_dn.wait_recv()
    l_up.wait_recv()
    l_dn.wait_recv()

    def x_sum(b):
        return part[row_of(x, b)] + from_lo[b].astype(F32) + from_hi[b].astype(F32)

    t_z = []
    for d in (1, 2, 3):
        z_send[d - 1] = rounded(x_sum(on(zl, d)))
        t_z.append(send(z_send.at[d - 1], z_recv.at[d - 1], L_TO[d - 1]))
    back = x_sum(zl)

    iy_up.wait_recv()
    ref = inputs.at[pl.ds(ym * 4, 2), core]
    if_up = send(ref, ref, Y_UP)
    iy_dn.wait_recv()
    ref = inputs.at[pl.ds(yp * 4 + 2, 2), core]
    if_dn = send(ref, ref, Y_DN)
    is_m = send(plane_core(inputs, ym, core), plane_core(inputs, ym, core), SIB)
    is_p = send(plane_core(inputs, yp, core), plane_core(inputs, yp, core), SIB)

    for d in (1, 2, 3):
        t_z[d - 1].wait_recv()
        back = back + z_recv[d - 1].astype(F32)
    back = back[:, 0:units]
    backs[row] = jnp.zeros((2, 64, WIDE), BF)
    backs[row, 0, :, 0:units] = rounded(back * upper * sig * (1.0 + gate * (1.0 - sig)))
    backs[row, 1, :, 0:units] = rounded(back * gate * sig)

    ref = backs.at[row]
    b_z = [send(ref, ref, where) for where in L_TO]

    def backs_x(b):
        ref = backs.at[row_of(x, b)]
        return send(ref, ref, X_UP), send(ref, ref, X_DN)

    bx = [backs_x(zl)]

    if_up.wait_recv()
    if_dn.wait_recv()
    is_o = send(plane_core(inputs, yo, core), plane_core(inputs, yo, core), SIB)

    def forward(ref, a, b, where):
        block = ref.at[row_of(a, b)]
        return send(block, block, where)

    bf = []
    for d in (1, 2, 3):
        b_z[d - 1].wait_recv()
        bx.append(backs_x(on(zl, -d)))
        if d == 1:
            bx[0][0].wait_recv()
            bf.append(forward(backs, xm, zl, X_UP))
        if d == 2:
            bx[1][1].wait_recv()
            bf.append(forward(backs, xp, on(zl, -1), X_DN))

    iy_s.wait_recv()
    is_m.wait_recv()
    is_p.wait_recv()
    is_o.wait_recv()

    sib_copies = []

    def use(a, first):
        gate_rows = backs[pl.ds(a * 4, 4), 0].reshape(256, WIDE)
        up_rows = backs[pl.ds(a * 4, 4), 1].reshape(256, WIDE)
        out = dot(gate_rows, wg[...], NN) + dot(up_rows, wu[...], NN)
        ipart[pl.ds(a * 4, 4)] = out.reshape(4, 2, 32, out.shape[1])
        sib_copies.append(send(plane_core(ipart, a, sib), plane(ipart_sib, a), SIB))
        in_rows = inputs[pl.ds(a * 4, 4)].reshape(256, inputs.shape[3])
        gate_sum, up_sum = dot(gate_rows, in_rows, TN), dot(up_rows, in_rows, TN)
        if first:
            gg_acc[...] = gate_sum
            ug_acc[...] = up_sum
        else:
            gg_acc[...] += gate_sum
            ug_acc[...] += up_sum

    use(x, True)
    bx[2][0].wait_recv()
    bf.append(forward(backs, xm, on(zl, -2), X_UP))
    bx[3][1].wait_recv()
    bf.append(forward(backs, xp, on(zl, -3), X_DN))
    bx[1][0].wait_recv()
    bx[3][0].wait_recv()
    use(xm, False)
    bx[0][1].wait_recv()
    bx[2][1].wait_recv()
    use(xp, False)
    for k in range(4):
        hx[k][0].wait_recv()
        hx[k][1].wait_recv()
    hf = [
        forward(hidden, xm, zl, X_UP),
        forward(hidden, xm, on(zl, -1), X_UP),
        forward(hidden, xp, on(zl, -2), X_DN),
        forward(hidden, xp, on(zl, -3), X_DN),
    ]
    for copy in bf:
        copy.wait_recv()
    use(xo, False)

    for copy in sib_copies:
        copy.wait_recv()
    for a in range(4):
        out = ipart[pl.ds(a * 4, 4), core] + ipart_sib[pl.ds(a * 4, 4)]
        iq[pl.ds(a * 4, 4)] = out
        iq_bf[pl.ds(a * 4, 4)] = rounded(out)

    q_up = send(two(iq_bf, yo, 0), ifar_lo, Y_UP)
    q_dn = send(two(iq_bf, yo, 2), ifar_hi, Y_DN)
    qe_up = send(two(iq_bf, yp, 2), ifrom_lo.at[pl.ds(2, 2)], Y_UP)
    qe_dn = send(two(iq_bf, ym, 0), ifrom_hi.at[pl.ds(0, 2)], Y_DN)

    gg[...] = rounded(gg_acc[0:units, :])
    ug[...] = rounded(ug_acc[0:units, :])
    c_gg = local(gg, gg_out)
    c_ug = local(ug, ug_out)

    q_up.wait_recv()
    iq_bf[pl.ds(yp * 4, 2)] = rounded(iq[pl.ds(yp * 4, 2)] + ifar_lo[...].astype(F32))
    ql_up = send(two(iq_bf, yp, 0), ifrom_lo.at[pl.ds(0, 2)], Y_UP)
    q_dn.wait_recv()
    iq_bf[pl.ds(ym * 4 + 2, 2)] = rounded(iq[pl.ds(ym * 4 + 2, 2)] + ifar_hi[...].astype(F32))
    ql_dn = send(two(iq_bf, ym, 2), ifrom_hi.at[pl.ds(2, 2)], Y_DN)

    for copy in hf:
        copy.wait_recv()
    h_rows = hidden[...].reshape(1024, WIDE)
    g_rows = grads[...].reshape(1024, grads.shape[3])
    dg[...] = rounded(dot(h_rows, g_rows, TN)[0:units, :])
    c_dg = local(dg, dg_out)

    qe_up.wait_recv()
    qe_dn.wait_recv()
    ql_up.wait_recv()
    ql_dn.wait_recv()

    def y_sum(b):
        return iq[row_of(y, b)] + ifrom_lo[b].astype(F32) + ifrom_hi[b].astype(F32)

    t_h = []
    for d, where in ((1, H_UP), (2, H_OP), (3, H_DN)):
        iz_send[d - 1] = rounded(y_sum(on(zh, d)))
        t_h.append(send(iz_send.at[d - 1], iz_recv.at[d - 1], where))
    total = y_sum(zh)
    for d in (1, 2, 3):
        t_h[d - 1].wait_recv()
        total = total + iz_recv[d - 1].astype(F32)
    ig[...] = rounded(total)
    c_ig = local(ig, ig_out)

    for copy in sent:
        copy.wait_send()
    for copy in (c_gg, c_ug, c_dg, c_ig):
        copy.wait()


def shards(out_grad, layer_input, gate_preact, up_preact, w_down, w_gate, w_up):
    tokens, feats = out_grad.shape
    units = gate_preact.shape[1]
    vm = pltpu.VMEM
    whole = (16, 2, 32, feats)
    ig, dg, gg, ug = pl.pallas_call(
        kernel,
        out_shape=(
            jax.ShapeDtypeStruct((tokens, feats), BF),
            jax.ShapeDtypeStruct((units, feats), BF),
            jax.ShapeDtypeStruct((units, feats), BF),
            jax.ShapeDtypeStruct((units, feats), BF),
        ),
        in_specs=[pl.BlockSpec(memory_space=pl.ANY)] * 7,
        out_specs=(pl.BlockSpec(memory_space=pl.ANY),) * 4,
        scratch_shapes=[
            vm(whole, BF), vm(whole, BF), vm((16, 64, WIDE), BF), vm((16, 2, 64, WIDE), BF),
            vm((64, units), BF), vm((64, units), BF),
            vm((units, feats), BF), vm((units, feats), BF), vm((units, feats), BF),
            vm((WIDE, feats), BF), vm((WIDE, feats), BF), vm((WIDE, feats), BF),
            vm((16, 64, WIDE), F32), vm((16, 64, WIDE), BF),
            vm((2, 64, WIDE), BF), vm((2, 64, WIDE), BF),
            vm((4, 64, WIDE), BF), vm((4, 64, WIDE), BF),
            vm((3, 64, WIDE), BF), vm((3, 64, WIDE), BF),
            vm(whole, F32), vm((16, 32, feats), F32),
            vm((16, 32, feats), F32), vm((16, 32, feats), BF),
            vm((2, 32, feats), BF), vm((2, 32, feats), BF),
            vm((4, 32, feats), BF), vm((4, 32, feats), BF),
            vm((3, 32, feats), BF), vm((3, 32, feats), BF),
            vm((WIDE, feats), F32), vm((WIDE, feats), F32),
            vm((units, feats), BF), vm((units, feats), BF), vm((units, feats), BF),
            vm((tokens, feats), BF),
            pltpu.SemaphoreType.DMA((16,)),
            pltpu.SemaphoreType.DMA((N_COPIES,)),
            pltpu.SemaphoreType.DMA((N_COPIES,)),
        ],
        compiler_params=pltpu.CompilerParams(
            collective_id=0, has_side_effects=True, vmem_limit_bytes=48 * 1024 * 1024
        ),
        cost_estimate=pl.CostEstimate(
            flops=12 * 1024 * units * feats, bytes_accessed=3_000_000, transcendentals=64 * units
        ),
        name="swiglu_back",
    )(out_grad, layer_input, gate_preact, up_preact, w_down.T, w_gate, w_up)
    return ig, dg.T, gg, ug


def solution(mesh):
    return jax.shard_map(
        shards,
        mesh=mesh,
        in_specs=(
            P("col", "row"),
            P("col", "row"),
            P("row", "col"),
            P("row", "col"),
            P("row", "col"),
            P("col", "row"),
            P("col", "row"),
        ),
        out_specs=(P("col", "row"), P("row", "col"), P("col", "row"), P("col", "row")),
        check_vma=False,
    )
```

```python
import jax
import jax.numpy as jnp
from jax import lax
from jax.experimental import pallas as pl
from jax.experimental.pallas import tpu as pltpu
from jax.sharding import PartitionSpec as P

BF = jnp.bfloat16
F32 = jnp.float32
MESH = pl.DeviceIdType.MESH
N_COPIES = 128
WIDE = 512
PARTS = 2
RT = 32 // PARTS
VMEM_ALL = 64 * 1024 * 1024 - 65536


def rounded(value):
    return value.astype(BF)


def dot(left, right, dims):
    return lax.dot_general(left, right, (dims, ((), ())), preferred_element_type=F32)


NN = ((1,), (0,))
NT = ((1,), (1,))
TN = ((0,), (0,))


def kernel(
    og_in, li_in, gp_in, up_in, wd_in, wg_in, wu_in,
    ig_out, dg_out, gg_out, ug_out,
    grads, inputs, hidden, backs, backs_sib,
    gp, up, pre, wd_raw, wg_raw, wu_raw, wd, wg, wu,
    part, part_bf, far_lo, far_hi, from_lo, from_hi, z_send, z_recv,
    iq, iq_bf, i_recv, iz_send, iz_recv,
    gg, ug, dg, ig,
    local_sem, send_sem, recv_sem,
):
    units = gp_in.shape[1]
    feats = og_in.shape[2]
    row, col = lax.axis_index("row"), lax.axis_index("col")
    x, zl = lax.div(row, 4), lax.rem(row, 4)
    y, zh, core = lax.div(col, 8), lax.rem(lax.div(col, 2), 4), lax.rem(col, 2)
    sib = 1 - core

    def on(value, step):
        return lax.rem(value + step + 4, 4)

    xp, xm, xo = on(x, 1), on(x, -1), on(x, 2)
    yp, ym, yo = on(y, 1), on(y, -1), on(y, 2)
    hp, hm, ho = on(zh, 1), on(zh, -1), on(zh, 2)

    def at(a, b):
        return a * 4 + b

    X_UP, X_DN = (at(xp, zl), col), (at(xm, zl), col)
    Y_UP, Y_DN, Y_OP = [(row, at(a, zh) * 2 + core) for a in (yp, ym, yo)]
    H_UP, H_DN, H_OP = [(row, at(y, b) * 2 + core) for b in (hp, hm, ho)]
    L_TO = [(at(x, on(zl, d)), col) for d in (1, 2, 3)]
    SIB = (row, at(y, zh) * 2 + sib)

    locals_ = []

    def local(src, dst):
        copy = pltpu.make_async_copy(src, dst, local_sem.at[len(locals_)])
        locals_.append(copy)
        copy.start()
        return copy

    sent = []

    def send(src, dst, where):
        k = len(sent)
        copy = pltpu.make_async_remote_copy(
            src_ref=src,
            dst_ref=dst,
            send_sem=send_sem.at[k],
            recv_sem=recv_sem.at[k],
            device_id=where,
            device_id_type=MESH,
        )
        copy.start()
        sent.append(copy)
        return copy

    def same(ref, where):
        return send(ref, ref, where)

    own = at(y, zh)
    c_og = local(og_in, grads.at[core, :, own])
    c_wd = local(wd_in, wd_raw)
    c_gp = local(gp_in, gp)
    c_up = local(up_in, up)
    c_wg = local(wg_in, wg_raw)
    c_wu = local(wu_in, wu_raw)
    c_li = local(li_in, inputs.at[core, :, own])

    barrier = pltpu.get_barrier_semaphore()
    partners = [X_UP, X_DN, Y_UP, Y_DN, Y_OP, H_UP, H_DN, H_OP, SIB] + L_TO
    for where in partners:
        pl.semaphore_signal(barrier, inc=1, device_id=where, device_id_type=MESH)
    pl.semaphore_wait(barrier, len(partners))

    def g(block):
        return grads.at[core, :, block]

    def gt(t, block):
        return grads.at[core, t, block]

    TO_H = ((ho, H_OP), (hm, H_UP), (hp, H_DN))
    TO_Y = (Y_OP, Y_UP, Y_DN)
    g_z = [[send(og_in.at[t], gt(t, own), where) for _, where in TO_H] for t in range(PARTS)]
    g_own = [send(og_in, g(own), where) for where in TO_Y]

    def padded(raw, ref, copy):
        copy.wait()
        ref[core, 0:units, :] = raw[...]
        ref[core, units:WIDE, :] = jnp.zeros((WIDE - units, feats), BF)
        return same(ref.at[core], SIB)

    s_wd = padded(wd_raw, wd, c_wd)
    c_gp.wait()
    c_up.wait()
    pre[core] = jnp.zeros((2, 2, 32, WIDE), BF)
    for half in (0, 1):
        pre[core, half, 0, :, 0:units] = gp[half * 32 : half * 32 + 32, :]
        pre[core, half, 1, :, 0:units] = up[half * 32 : half * 32 + 32, :]
    s_pre = same(pre.at[core, sib], SIB)
    for half in (0, 1):
        gate = pre[core, half, 0].astype(F32)
        value = rounded(gate * jax.nn.sigmoid(gate) * pre[core, half, 1].astype(F32))
        hidden[half, :, row] = value.reshape(PARTS, RT, WIDE)

    def h(block):
        return hidden.at[:, :, block]

    hx = [(same(h(row), X_UP), same(h(row), X_DN))]

    g_y = []
    for t in range(PARTS):
        copies = []
        for k in (1, 2, 0):
            g_z[t][k].wait_recv()
            block = gt(t, at(y, TO_H[k][0]))
            copies += [same(block, where) for where in TO_Y]
        g_y.append(copies)

    def li(block):
        return inputs.at[core, :, block]

    i_z = [send(li_in, li(own), where) for _, where in TO_H]
    h_z = [same(h(row), where) for where in L_TO]

    def partial(t, a):
        rows = grads[core, t, pl.ds(a * 4, 4)].reshape(4 * RT, feats)
        for j in (0, 1):
            out = dot(rows, wd[j], NT).reshape(4, RT, WIDE)
            part[t, pl.ds(a * 4, 4), j] = out
            part_bf[t, pl.ds(a * 4, 4), j] = rounded(out)

    def two(ref, t, a, b):
        return ref.at[t, pl.ds(a * 4 + b, 2)]

    def far(t):
        return (
            send(two(part_bf, t, xo, 0), far_lo.at[t], X_UP),
            send(two(part_bf, t, xo, 2), far_hi.at[t], X_DN),
        )

    def early(t):
        return (
            send(two(part_bf, t, xp, 2), from_lo.at[t, pl.ds(2, 2)], X_UP),
            send(two(part_bf, t, xm, 0), from_hi.at[t, pl.ds(0, 2)], X_DN),
        )

    def late(t, arrived):
        arrived[0].wait_recv()
        lo = pl.ds(xp * 4, 2)
        part_bf[t, lo] = rounded(part[t, lo] + far_lo[t].astype(F32))
        up_copy = send(two(part_bf, t, xp, 0), from_lo.at[t, pl.ds(0, 2)], X_UP)
        arrived[1].wait_recv()
        hi = pl.ds(xm * 4 + 2, 2)
        part_bf[t, hi] = rounded(part[t, hi] + far_hi[t].astype(F32))
        return up_copy, send(two(part_bf, t, xm, 2), from_hi.at[t, pl.ds(2, 2)], X_DN)

    def along_z(t, copies):
        for copy in copies:
            copy.wait_recv()

        def x_sum(b):
            return part[t, at(x, b)] + from_lo[t, b].astype(F32) + from_hi[t, b].astype(F32)

        out = []
        for d in (1, 2, 3):
            z_send[t, d - 1] = rounded(x_sum(on(zl, d)))
            out.append(send(z_send.at[t, d - 1], z_recv.at[t, d - 1], L_TO[d - 1]))
        return out, x_sum(zl)

    c_og.wait()
    s_wd.wait_recv()
    for copy in g_own:
        copy.wait_recv()

    def begin(t):
        for copy in g_y[t]:
            copy.wait_recv()
        partial(t, xo)
        first = far(t)
        partial(t, xp)
        partial(t, xm)
        return first

    r0 = begin(0)
    e0 = early(0)
    partial(0, x)
    r1 = begin(1)
    l0 = late(0, r0)
    e1 = early(1)
    partial(1, x)
    l1 = late(1, r1)
    s_g = same(grads.at[core], SIB)
    s_wg = padded(wg_raw, wg, c_wg)
    s_wu = padded(wu_raw, wu, c_wu)

    for copy in i_z:
        copy.wait_recv()
    c_li.wait()
    ref = inputs.at[core, :, pl.ds(y * 4, 4)]
    i_y = [same(ref, where) for where in TO_Y]

    t0, back0 = along_z(0, e0 + l0)
    for d in (1, 2, 3):
        h_z[d - 1].wait_recv()
        block = h(at(x, on(zl, -d)))
        hx.append((same(block, X_UP), same(block, X_DN)))
    t1, back1 = along_z(1, e1 + l1)
    s_pre.wait_recv()

    def b_ref(t, a, b):
        return backs.at[t, at(a, b)]

    def start_backs(t, back, copies):
        for d in (1, 2, 3):
            copies[d - 1].wait_recv()
            back = back + z_recv[t, d - 1].astype(F32)
        for j in (0, 1):
            rows = pl.ds(t * RT, RT)
            gate = pre[j, core, 0, rows].astype(F32)
            upper = pre[j, core, 1, rows].astype(F32)
            sig = jax.nn.sigmoid(gate)
            backs[t, row, 0, j] = rounded(back[j] * upper * sig * (1.0 + gate * (1.0 - sig)))
            backs[t, row, 1, j] = rounded(back[j] * gate * sig)
        ref = backs.at[t, row]
        return [same(ref, X_UP)], [same(ref, X_DN)], [same(ref, where) for where in L_TO]

    bu0, bd0, bz0 = start_backs(0, back0, t0)
    bu1, bd1, bz1 = start_backs(1, back1, t1)

    for copy in i_y:
        copy.wait_recv()
    s_i = same(inputs.at[core], SIB)

    def from_z(t, bu, bd, bz, d):
        bz[d - 1].wait_recv()
        ref = b_ref(t, x, on(zl, -d))
        bu.append(same(ref, X_UP))
        bd.append(same(ref, X_DN))

    def forward(t, copy, a, b, where):
        copy.wait_recv()
        return same(b_ref(t, a, b), where)

    s_b = []

    def use(t, a):
        total = None
        for k, weight in ((0, wg), (1, wu)):
            for j in (0, 1):
                rows = backs[t, pl.ds(a * 4, 4), k, j].reshape(4 * RT, WIDE)
                term = dot(rows, weight[j], NN)
                total = term if total is None else total + term
        out = total.reshape(4, RT, feats)
        iq[t, pl.ds(a * 4, 4)] = out
        iq_bf[t, pl.ds(a * 4, 4)] = rounded(out)
        some = pl.ds(a * 4, 4)
        s_b.append(send(backs.at[t, some, :, sib], backs_sib.at[t, some], SIB))

    def plane(ref, t, a):
        return ref.at[t, pl.ds(a * 4, 4)]

    def along_y(t):
        return [
            send(plane(iq_bf, t, a), i_recv.at[t, k], where)
            for k, (a, where) in enumerate(((yo, Y_OP), (yp, Y_UP), (ym, Y_DN)))
        ]

    def along_h(t, copies):
        for copy in copies:
            copy.wait_recv()

        def y_sum(b):
            out = iq[t, at(y, b)]
            for k in range(3):
                out = out + i_recv[t, k, b].astype(F32)
            return out

        out = []
        for k, (b, where) in enumerate(((ho, H_OP), (hp, H_UP), (hm, H_DN))):
            iz_send[t, k] = rounded(y_sum(b))
            out.append(send(iz_send.at[t, k], iz_recv.at[t, k], where))
        return out, y_sum(zh)

    def finish(t, copies, total):
        for k in range(3):
            copies[k].wait_recv()
            total = total + iz_recv[t, k].astype(F32)
        ig[t] = rounded(total)

    bf0, bf1 = [], []
    from_z(0, bu0, bd0, bz0, 1)
    bf0.append(forward(0, bu0[0], xm, zl, X_UP))
    from_z(0, bu0, bd0, bz0, 2)
    bf1.append(forward(1, bu1[0], xm, zl, X_UP))
    from_z(0, bu0, bd0, bz0, 3)
    s_wg.wait_recv()
    s_wu.wait_recv()
    use(0, x)
    bf0.append(forward(0, bd0[1], xp, on(zl, -1), X_DN))
    from_z(1, bu1, bd1, bz1, 1)
    bf0.append(forward(0, bu0[2], xm, on(zl, -2), X_UP))
    from_z(1, bu1, bd1, bz1, 2)
    bf0.append(forward(0, bd0[3], xp, on(zl, -3), X_DN))
    from_z(1, bu1, bd1, bz1, 3)
    bu0[1].wait_recv()
    bu0[3].wait_recv()
    use(0, xm)
    bf1.append(forward(1, bd1[1], xp, on(zl, -1), X_DN))
    bd0[0].wait_recv()
    bd0[2].wait_recv()
    use(0, xp)
    bf1.append(forward(1, bu1[2], xm, on(zl, -2), X_UP))
    use(1, x)
    for copy in bf0:
        copy.wait_recv()
    use(0, xo)
    q0 = along_y(0)
    bf1.append(forward(1, bd1[3], xp, on(zl, -3), X_DN))

    for k in range(4):
        hx[k][0].wait_recv()
        hx[k][1].wait_recv()
    hf = [
        same(h(at(xm, zl)), X_UP),
        same(h(at(xm, on(zl, -1))), X_UP),
        same(h(at(xp, on(zl, -2))), X_DN),
        same(h(at(xp, on(zl, -3))), X_DN),
    ]

    bu1[1].wait_recv()
    bu1[3].wait_recv()
    use(1, xm)
    bd1[0].wait_recv()
    bd1[2].wait_recv()
    use(1, xp)
    z0, total0 = along_h(0, q0)
    for copy in bf1:
        copy.wait_recv()
    use(1, xo)
    q1 = along_y(1)

    def tokens(value):
        return value.reshape(512, value.shape[-1])

    for copy in hf:
        copy.wait_recv()
    s_g.wait_recv()
    dg[...] = rounded(
        dot(hidden[...].reshape(1024, WIDE), grads[...].reshape(1024, feats), TN)[0:units, :]
    )
    outs = [local(dg, dg_out)]
    z1, total1 = along_h(1, q1)
    finish(0, z0, total0)
    s_i.wait_recv()
    for copy in s_b:
        copy.wait_recv()
    for k, ref, out in ((0, gg, gg_out), (1, ug, ug_out)):
        value = dot(tokens(backs[:, :, k, core]), tokens(inputs[core]), TN)
        value = value + dot(tokens(backs_sib[:, :, k]), tokens(inputs[sib]), TN)
        ref[...] = rounded(value[0:units, :])
        outs.append(local(ref, out))
    finish(1, z1, total1)
    outs.append(local(ig, ig_out))

    for copy in sent:
        copy.wait_send()
    for copy in outs:
        copy.wait()


def hand_over(*refs):
    sources, targets, rooms, sem = refs[:4], refs[4:8], refs[8:12], refs[12]
    into = [pltpu.make_async_copy(s, v, sem.at[k]) for k, (s, v) in enumerate(zip(sources, rooms))]
    out = [pltpu.make_async_copy(v, t, sem.at[4 + k]) for k, (v, t) in enumerate(zip(rooms, targets))]
    for copy in into:
        copy.start()
    for first, second in zip(into, out):
        first.wait()
        second.start()
    for copy in out:
        copy.wait()


def shards(out_grad, layer_input, gate_preact, up_preact, w_down, w_gate, w_up):
    tokens, feats = out_grad.shape
    units = gate_preact.shape[1]
    vm = pltpu.VMEM
    any_space = pl.BlockSpec(memory_space=pl.ANY)
    shapes = (
        jax.ShapeDtypeStruct((PARTS, RT, feats), BF),
        jax.ShapeDtypeStruct((units, feats), BF),
        jax.ShapeDtypeStruct((units, feats), BF),
        jax.ShapeDtypeStruct((units, feats), BF),
    )
    results = pl.pallas_call(
        kernel,
        out_shape=shapes,
        in_specs=[any_space] * 7,
        out_specs=(any_space,) * 4,
        scratch_shapes=[
            vm((2, PARTS, 16, RT, feats), BF),
            vm((2, PARTS, 16, RT, feats), BF),
            vm((2, PARTS, 16, RT, WIDE), BF),
            vm((PARTS, 16, 2, 2, RT, WIDE), BF),
            vm((PARTS, 16, 2, RT, WIDE), BF),
            vm((64, units), BF), vm((64, units), BF), vm((2, 2, 2, 32, WIDE), BF),
            vm((units, feats), BF), vm((units, feats), BF), vm((units, feats), BF),
            vm((2, WIDE, feats), BF), vm((2, WIDE, feats), BF), vm((2, WIDE, feats), BF),
            vm((PARTS, 16, 2, RT, WIDE), F32), vm((PARTS, 16, 2, RT, WIDE), BF),
            vm((PARTS, 2, 2, RT, WIDE), BF), vm((PARTS, 2, 2, RT, WIDE), BF),
            vm((PARTS, 4, 2, RT, WIDE), BF), vm((PARTS, 4, 2, RT, WIDE), BF),
            vm((PARTS, 3, 2, RT, WIDE), BF), vm((PARTS, 3, 2, RT, WIDE), BF),
            vm((PARTS, 16, RT, feats), F32), vm((PARTS, 16, RT, feats), BF),
            vm((PARTS, 3, 4, RT, feats), BF),
            vm((PARTS, 3, RT, feats), BF), vm((PARTS, 3, RT, feats), BF),
            vm((units, feats), BF), vm((units, feats), BF), vm((units, feats), BF),
            vm((PARTS, RT, feats), BF),
            pltpu.SemaphoreType.DMA((16,)),
            pltpu.SemaphoreType.DMA((N_COPIES,)),
            pltpu.SemaphoreType.DMA((N_COPIES,)),
        ],
        compiler_params=pltpu.CompilerParams(
            collective_id=0, has_side_effects=True, vmem_limit_bytes=VMEM_ALL
        ),
        cost_estimate=pl.CostEstimate(
            flops=12 * 1024 * units * feats, bytes_accessed=3_000_000, transcendentals=64 * units
        ),
        name="swiglu_back",
    )(
        out_grad.reshape(PARTS, RT, feats),
        layer_input.reshape(PARTS, RT, feats),
        gate_preact,
        up_preact,
        w_down.T,
        w_gate,
        w_up,
    )
    ig, dg, gg, ug = pl.pallas_call(
        hand_over,
        out_shape=shapes,
        in_specs=[any_space] * 4,
        out_specs=(any_space,) * 4,
        scratch_shapes=[vm(s.shape, s.dtype) for s in shapes] + [pltpu.SemaphoreType.DMA((8,))],
        compiler_params=pltpu.CompilerParams(vmem_limit_bytes=VMEM_ALL),
        name="hand_over",
    )(*results)
    return ig.reshape(tokens, feats), dg.T, gg, ug


def solution(mesh):
    return jax.shard_map(
        shards,
        mesh=mesh,
        in_specs=(
            P("col", "row"),
            P("col", "row"),
            P("row", "col"),
            P("row", "col"),
            P("row", "col"),
            P("col", "row"),
            P("col", "row"),
        ),
        out_specs=(P("col", "row"), P("row", "col"), P("col", "row"), P("col", "row")),
        check_vma=False,
    )
```

```python
import jax
import jax.numpy as jnp
from jax import lax
from jax.experimental import pallas as pl
from jax.experimental.pallas import tpu as pltpu
from jax.sharding import PartitionSpec as P

BF = jnp.bfloat16
F32 = jnp.float32
MESH = pl.DeviceIdType.MESH
N_GROUPS = 7
N_ARRIVALS = 60
WIDE = 512
PARTS = 2
RT = 32 // PARTS
VMEM_ALL = 64 * 1024 * 1024 - 65536


def rounded(value):
    return value.astype(BF)


def dot(left, right, dims):
    return lax.dot_general(left, right, (dims, ((), ())), preferred_element_type=F32)


NN = ((1,), (0,))
NT = ((1,), (1,))
TN = ((0,), (0,))


def kernel(
    og_in, li_in, gp_in, up_in, wd_in, wg_in, wu_in,
    ig_out, dg_out, gg_out, ug_out,
    grads, inputs, hidden, backs, backs_sib,
    gp, up, pre, wd_raw, wg_raw, wu_raw, wd, wg, wu,
    part, part_bf, far_lo, far_hi, from_lo, from_hi, z_send, z_recv,
    iq, iq_bf, i_recv, iz_send, iz_recv,
    gg, ug, dg, ig,
    local_sem, send_sem, recv_sem,
):
    units = gp_in.shape[1]
    feats = og_in.shape[2]
    row, col = lax.axis_index("row"), lax.axis_index("col")
    x, zl = lax.div(row, 4), lax.rem(row, 4)
    y, zh, core = lax.div(col, 8), lax.rem(lax.div(col, 2), 4), lax.rem(col, 2)
    sib = 1 - core

    def on(value, step):
        return lax.rem(value + step + 4, 4)

    xp, xm, xo = on(x, 1), on(x, -1), on(x, 2)
    yp, ym, yo = on(y, 1), on(y, -1), on(y, 2)
    hp, hm, ho = on(zh, 1), on(zh, -1), on(zh, 2)

    def at(a, b):
        return a * 4 + b

    X_UP, X_DN, X_OP = [(at(a, zl), col) for a in (xp, xm, xo)]
    Y_UP, Y_DN, Y_OP = [(row, at(a, zh) * 2 + core) for a in (yp, ym, yo)]
    H_UP, H_DN, H_OP = [(row, at(y, b) * 2 + core) for b in (hp, hm, ho)]
    L_TO = [(at(x, on(zl, d)), col) for d in (1, 2, 3)]
    SIB = (row, at(y, zh) * 2 + sib)

    locals_ = []

    def local(src, dst):
        copy = pltpu.make_async_copy(src, dst, local_sem.at[len(locals_)])
        locals_.append(copy)
        copy.start()
        return copy

    arrivals = []

    def arrival():
        arrivals.append(recv_sem.at[len(arrivals)])
        return arrivals[-1]

    def remote(src, dst, where, group, arrived):
        return pltpu.make_async_remote_copy(
            src_ref=src,
            dst_ref=dst,
            send_sem=send_sem.at[group],
            recv_sem=arrived,
            device_id=where,
            device_id_type=MESH,
        )

    def send(src, dst, where, group, arrived):
        remote(src, dst, where, group, arrived).start()

    def same(ref, where, group, arrived):
        remote(ref, ref, where, group, arrived).start()

    def wait(arrived, like):
        remote(like, like, SIB, 0, arrived).wait_recv()

    def wait_sent(group, like):
        remote(like, like, SIB, group, arrivals[0]).wait_send()

    OUT_A, OUT_W, OUT_H, OUT_B, OUT_C, OUT_S, OUT_D = range(N_GROUPS)

    own = at(y, zh)
    c_og = local(og_in, grads.at[core, :, own])
    c_wd = local(wd_in, wd_raw)
    c_gp = local(gp_in, gp)
    c_up = local(up_in, up)
    c_wg = local(wg_in, wg_raw)
    c_wu = local(wu_in, wu_raw)
    c_li = local(li_in, inputs.at[core, :, own])

    barrier = pltpu.get_barrier_semaphore()
    partners = [X_UP, X_DN, X_OP, Y_UP, Y_DN, Y_OP, H_UP, H_DN, H_OP, SIB] + L_TO
    for where in partners:
        pl.semaphore_signal(barrier, inc=1, device_id=where, device_id_type=MESH)
    pl.semaphore_wait(barrier, len(partners))

    def g(block):
        return grads.at[core, :, block]

    def gt(t, block):
        return grads.at[core, t, block]

    TO_H = ((ho, H_OP), (hm, H_UP), (hp, H_DN))
    TO_Y = (Y_OP, Y_UP, Y_DN)
    g_z = [[arrival() for _ in range(3)] for _ in range(PARTS)]
    g_own = arrival()
    for t in range(PARTS):
        for k in range(3):
            send(og_in.at[t], gt(t, own), TO_H[k][1], OUT_A, g_z[t][k])
    for where in TO_Y:
        send(og_in, g(own), where, OUT_A, g_own)

    def padded(raw, ref, copy):
        copy.wait()
        ref[core, 0:units, :] = raw[...]
        ref[core, units:WIDE, :] = jnp.zeros((WIDE - units, feats), BF)
        arrived = arrival()
        same(ref.at[core], SIB, OUT_W, arrived)
        return arrived

    s_wd = padded(wd_raw, wd, c_wd)
    c_gp.wait()
    c_up.wait()
    pre[core] = jnp.zeros((2, 2, 32, WIDE), BF)
    for half in (0, 1):
        pre[core, half, 0, :, 0:units] = gp[half * 32 : half * 32 + 32, :]
        pre[core, half, 1, :, 0:units] = up[half * 32 : half * 32 + 32, :]
    s_pre = arrival()
    same(pre.at[core, sib], SIB, OUT_H, s_pre)
    for half in (0, 1):
        gate = pre[core, half, 0].astype(F32)
        value = rounded(gate * jax.nn.sigmoid(gate) * pre[core, half, 1].astype(F32))
        hidden[half, :, row] = value.reshape(PARTS, RT, WIDE)

    def h(block):
        return hidden.at[:, :, block]

    h_x, h_z = arrival(), arrival()
    for where in (X_OP, X_UP, X_DN):
        same(h(row), where, OUT_H, h_x)

    g_y = [arrival() for _ in range(PARTS)]
    for t in range(PARTS):
        for k in (1, 2, 0):
            block = gt(t, at(y, TO_H[k][0]))
            wait(g_z[t][k], block)
            for where in TO_Y:
                same(block, where, OUT_A, g_y[t])

    def li(block):
        return inputs.at[core, :, block]

    i_z = arrival()
    for _, where in TO_H:
        send(li_in, li(own), where, OUT_A, i_z)

    def partial(t, j):
        rows = grads[core, t].reshape(16 * RT, feats)
        out = dot(rows, wd[j], NT).reshape(16, RT, WIDE)
        part[t * 2 + j] = out
        part_bf[t * 2 + j] = rounded(out)

    def two(ref, u, a, b):
        return ref.at[u, pl.ds(a * 4 + b, 2)]

    n_units = 2 * PARTS
    r_up = [arrival() for _ in range(n_units)]
    r_dn = [arrival() for _ in range(n_units)]
    x_in = [arrival() for _ in range(n_units)]
    z_in = [arrival() for _ in range(n_units)]

    def begin(u):
        send(two(part_bf, u, xo, 0), far_lo.at[u], X_UP, OUT_B, r_up[u])
        send(two(part_bf, u, xo, 2), far_hi.at[u], X_DN, OUT_B, r_dn[u])
        send(two(part_bf, u, xp, 2), from_lo.at[u, pl.ds(2, 2)], X_UP, OUT_B, x_in[u])
        send(two(part_bf, u, xm, 0), from_hi.at[u, pl.ds(0, 2)], X_DN, OUT_B, x_in[u])

    def late(u):
        wait(r_up[u], far_lo.at[u])
        lo = pl.ds(xp * 4, 2)
        part_bf[u, lo] = rounded(part[u, lo] + far_lo[u].astype(F32))
        send(two(part_bf, u, xp, 0), from_lo.at[u, pl.ds(0, 2)], X_UP, OUT_B, x_in[u])
        wait(r_dn[u], far_hi.at[u])
        hi = pl.ds(xm * 4 + 2, 2)
        part_bf[u, hi] = rounded(part[u, hi] + far_hi[u].astype(F32))
        send(two(part_bf, u, xm, 2), from_hi.at[u, pl.ds(2, 2)], X_DN, OUT_B, x_in[u])

    def x_sum(u, b):
        return part[u, at(x, b)] + from_lo[u, b].astype(F32) + from_hi[u, b].astype(F32)

    def along_z(u):
        wait(x_in[u], part_bf.at[u, pl.ds(0, 8)])
        for d in (2, 1, 3):
            z_send[u, d - 1] = rounded(x_sum(u, on(zl, d)))
            send(z_send.at[u, d - 1], z_recv.at[u, d - 1], L_TO[d - 1], OUT_B, z_in[u])

    c_og.wait()
    wait(s_wd, wd.at[sib])
    wait(g_own, grads.at[0, :, pl.ds(0, 3)])
    wait(g_y[0], grads.at[0, 0, pl.ds(0, 9)])
    partial(0, 0)
    begin(0)
    partial(0, 1)
    begin(1)
    late(0)
    wait(g_y[1], grads.at[0, 0, pl.ds(0, 9)])
    partial(1, 0)
    begin(2)
    late(1)
    partial(1, 1)
    begin(3)
    along_z(0)
    late(2)
    along_z(1)
    late(3)
    s_g = arrival()
    same(grads.at[core], SIB, OUT_W, s_g)
    s_wg = padded(wg_raw, wg, c_wg)
    s_wu = padded(wu_raw, wu, c_wu)
    along_z(2)

    along_z(3)
    wait(s_pre, pre.at[sib, core])

    def b_ref(t, a, b):
        return backs.at[t, at(a, b)]

    b_z = [[arrival() for _ in range(3)] for _ in range(PARTS)]
    b_one = [[arrival() for _ in range(4)] for _ in range(PARTS)]
    b_up = [arrival() for _ in range(PARTS)]
    b_dn = [arrival() for _ in range(PARTS)]
    b_far = [arrival() for _ in range(PARTS)]

    def backs_x(t, d):
        ref = b_ref(t, x, on(zl, -d))
        same(ref, X_UP, OUT_C, {2: b_one[t][0], 3: b_one[t][1]}.get(d, b_up[t]))
        same(ref, X_DN, OUT_C, {1: b_one[t][2], 3: b_one[t][3]}.get(d, b_dn[t]))

    def start_backs(t):
        for j in (0, 1):
            u = t * 2 + j
            wait(z_in[u], z_recv.at[u])
            back = x_sum(u, zl)
            for d in (1, 2, 3):
                back = back + z_recv[u, d - 1].astype(F32)
            rows = pl.ds(t * RT, RT)
            gate = pre[j, core, 0, rows].astype(F32)
            upper = pre[j, core, 1, rows].astype(F32)
            sig = jax.nn.sigmoid(gate)
            backs[t, row, 0, j] = rounded(back * upper * sig * (1.0 + gate * (1.0 - sig)))
            backs[t, row, 1, j] = rounded(back * gate * sig)
        for d in (2, 1, 3):
            same(backs.at[t, row], L_TO[d - 1], OUT_C, b_z[t][d - 1])
        same(backs.at[t, row], X_OP, OUT_C, b_far[t])
        backs_x(t, 0)

    start_backs(0)

    wait(i_z, inputs.at[0, :, pl.ds(0, 3)])
    c_li.wait()
    i_y = arrival()
    for where in TO_Y:
        same(inputs.at[core, :, pl.ds(y * 4, 4)], where, OUT_H, i_y)
    start_backs(1)

    def from_z(t, d):
        wait(b_z[t][d - 1], b_ref(t, x, on(zl, -d)))
        backs_x(t, d)

    def forward(t, d):
        up_ref, dn_ref = b_ref(t, xm, on(zl, -d)), b_ref(t, xp, on(zl, -d))
        if d == 2:
            wait(b_one[t][0], up_ref)
            same(up_ref, X_UP, OUT_C, b_far[t])
        elif d == 1:
            wait(b_one[t][2], dn_ref)
            same(dn_ref, X_DN, OUT_C, b_far[t])
        else:
            wait(b_one[t][1], up_ref)
            same(up_ref.at[0], X_UP, OUT_C, b_far[t])
            wait(b_one[t][3], dn_ref)
            same(dn_ref.at[1], X_DN, OUT_C, b_far[t])

    s_b = arrival()
    q_y = [arrival() for _ in range(PARTS)]
    q_z = [arrival() for _ in range(PARTS)]

    def to_y(t, a):
        @pl.when(a != y)
        def _():
            where = (row, at(a, zh) * 2 + core)
            send(iq_bf.at[t, pl.ds(a * 4, 4)], i_recv.at[t, y], where, OUT_D, q_y[t])

    def use(t, planes):
        total = None
        for k, weight in ((0, wg), (1, wu)):
            for j in (0, 1):
                rows = [backs[t, pl.ds(a * 4, 4), k, j].reshape(4 * RT, WIDE) for a in planes]
                rows = rows[0] if len(rows) == 1 else jnp.concatenate(rows, axis=0)
                term = dot(rows, weight[j], NN)
                total = term if total is None else total + term
        for k, a in enumerate(planes):
            out = total[k * 4 * RT : (k + 1) * 4 * RT].reshape(4, RT, feats)
            some = pl.ds(a * 4, 4)
            iq[t, some] = out
            iq_bf[t, some] = rounded(out)
            to_y(t, a)
            send(backs.at[t, some, :, sib], backs_sib.at[t, some], SIB, OUT_S, s_b)

    def y_sum(t, b):
        out = iq[t, at(y, b)]
        for k in range(3):
            out = out + i_recv[t, on(y, k + 1), b].astype(F32)
        return out

    def along_h(t):
        wait(q_y[t], i_recv.at[t, pl.ds(0, 3)])
        for k, (b, where) in enumerate(((ho, H_OP), (hp, H_UP), (hm, H_DN))):
            iz_send[t, k] = rounded(y_sum(t, b))
            send(iz_send.at[t, k], iz_recv.at[t, k], where, OUT_D, q_z[t])

    def finish(t):
        wait(q_z[t], iz_recv.at[t])
        total = y_sum(t, zh)
        for k in range(3):
            total = total + iz_recv[t, k].astype(F32)
        ig[t] = rounded(total)

    for t in range(PARTS):
        for d in (2, 1, 3):
            from_z(t, d)

    for where in L_TO:
        same(h(row), where, OUT_H, h_z)
    wait(s_wg, wg.at[sib])
    wait(s_wu, wu.at[sib])
    forward(0, 2)
    forward(0, 1)
    forward(0, 3)
    forward(1, 2)
    wait(b_up[0], backs.at[0, pl.ds(0, 2)])
    wait(b_dn[0], backs.at[0, pl.ds(0, 2)])
    use(0, (x, xm, xp))
    forward(1, 1)
    forward(1, 3)
    wait(b_far[0], backs.at[0, pl.ds(0, 4)])
    use(0, (xo,))
    wait(h_z, hidden.at[:, :, pl.ds(0, 3)])
    for d in (1, 2, 3):
        for where in (X_OP, X_UP, X_DN):
            same(h(at(x, on(zl, -d))), where, OUT_H, h_x)
    wait(i_y, inputs.at[0, :, pl.ds(0, 12)])
    s_i = arrival()
    same(inputs.at[core], SIB, OUT_H, s_i)

    wait(b_up[1], backs.at[1, pl.ds(0, 2)])
    wait(b_dn[1], backs.at[1, pl.ds(0, 2)])
    use(1, (x, xm, xp))
    along_h(0)
    wait(b_far[1], backs.at[1, pl.ds(0, 4)])
    use(1, (xo,))
    along_h(1)

    def tokens(value):
        return value.reshape(512, value.shape[-1])

    wait(s_i, inputs.at[sib])
    wait(s_b, backs_sib)
    outs = []
    for k, ref, out in ((0, gg, gg_out), (1, ug, ug_out)):
        value = dot(tokens(backs[:, :, k, core]), tokens(inputs[core]), TN)
        value = value + dot(tokens(backs_sib[:, :, k]), tokens(inputs[sib]), TN)
        ref[...] = rounded(value[0:units, :])
        outs.append(local(ref, out))
    finish(0)
    wait(h_x, hidden.at[:, :, pl.ds(0, 12)])
    wait(s_g, grads.at[sib])
    dg[...] = rounded(
        dot(hidden[...].reshape(1024, WIDE), grads[...].reshape(1024, feats), TN)[0:units, :]
    )
    outs.append(local(dg, dg_out))
    finish(1)
    outs.append(local(ig, ig_out))

    wait_sent(OUT_A, grads.at[:, :, pl.ds(0, 9)])
    wait_sent(OUT_W, backs)
    wait_sent(OUT_H, backs.at[:, pl.ds(0, 15)])
    wait_sent(OUT_B, grads.at[:, :, pl.ds(0, 15)])
    wait_sent(OUT_C, backs.at[:, pl.ds(0, 15)])
    wait_sent(OUT_S, backs.at[0])
    wait_sent(OUT_D, grads.at[0, :, pl.ds(0, 15)])
    for copy in outs:
        copy.wait()
    assert len(arrivals) == N_ARRIVALS, len(arrivals)


def hand_over(*refs):
    sources, targets, rooms, sem = refs[:4], refs[4:8], refs[8:12], refs[12]
    into = [pltpu.make_async_copy(s, v, sem.at[k]) for k, (s, v) in enumerate(zip(sources, rooms))]
    out = [pltpu.make_async_copy(v, t, sem.at[4 + k]) for k, (v, t) in enumerate(zip(rooms, targets))]
    for copy in into:
        copy.start()
    for first, second in zip(into, out):
        first.wait()
        second.start()
    for copy in out:
        copy.wait()


def shards(out_grad, layer_input, gate_preact, up_preact, w_down, w_gate, w_up):
    tokens, feats = out_grad.shape
    units = gate_preact.shape[1]
    vm = pltpu.VMEM
    any_space = pl.BlockSpec(memory_space=pl.ANY)
    shapes = (
        jax.ShapeDtypeStruct((PARTS, RT, feats), BF),
        jax.ShapeDtypeStruct((units, feats), BF),
        jax.ShapeDtypeStruct((units, feats), BF),
        jax.ShapeDtypeStruct((units, feats), BF),
    )
    results = pl.pallas_call(
        kernel,
        out_shape=shapes,
        in_specs=[any_space] * 7,
        out_specs=(any_space,) * 4,
        scratch_shapes=[
            vm((2, PARTS, 16, RT, feats), BF),
            vm((2, PARTS, 16, RT, feats), BF),
            vm((2, PARTS, 16, RT, WIDE), BF),
            vm((PARTS, 16, 2, 2, RT, WIDE), BF),
            vm((PARTS, 16, 2, RT, WIDE), BF),
            vm((64, units), BF), vm((64, units), BF), vm((2, 2, 2, 32, WIDE), BF),
            vm((units, feats), BF), vm((units, feats), BF), vm((units, feats), BF),
            vm((2, WIDE, feats), BF), vm((2, WIDE, feats), BF), vm((2, WIDE, feats), BF),
            vm((2 * PARTS, 16, RT, WIDE), F32), vm((2 * PARTS, 16, RT, WIDE), BF),
            vm((2 * PARTS, 2, RT, WIDE), BF), vm((2 * PARTS, 2, RT, WIDE), BF),
            vm((2 * PARTS, 4, RT, WIDE), BF), vm((2 * PARTS, 4, RT, WIDE), BF),
            vm((2 * PARTS, 3, RT, WIDE), BF), vm((2 * PARTS, 3, RT, WIDE), BF),
            vm((PARTS, 16, RT, feats), F32), vm((PARTS, 16, RT, feats), BF),
            vm((PARTS, 4, 4, RT, feats), BF),
            vm((PARTS, 3, RT, feats), BF), vm((PARTS, 3, RT, feats), BF),
            vm((units, feats), BF), vm((units, feats), BF), vm((units, feats), BF),
            vm((PARTS, RT, feats), BF),
            pltpu.SemaphoreType.DMA((11,)),
            pltpu.SemaphoreType.DMA((N_GROUPS,)),
            pltpu.SemaphoreType.DMA((N_ARRIVALS,)),
        ],
        compiler_params=pltpu.CompilerParams(
            collective_id=0, has_side_effects=True, vmem_limit_bytes=VMEM_ALL
        ),
        cost_estimate=pl.CostEstimate(
            flops=12 * 1024 * units * feats, bytes_accessed=3_000_000, transcendentals=64 * units
        ),
        name="swiglu_back",
    )(
        out_grad.reshape(PARTS, RT, feats),
        layer_input.reshape(PARTS, RT, feats),
        gate_preact,
        up_preact,
        w_down.T,
        w_gate,
        w_up,
    )
    ig, dg, gg, ug = pl.pallas_call(
        hand_over,
        out_shape=shapes,
        in_specs=[any_space] * 4,
        out_specs=(any_space,) * 4,
        scratch_shapes=[vm(s.shape, s.dtype) for s in shapes] + [pltpu.SemaphoreType.DMA((8,))],
        compiler_params=pltpu.CompilerParams(vmem_limit_bytes=VMEM_ALL),
        name="hand_over",
    )(*results)
    return ig.reshape(tokens, feats), dg.T, gg, ug


def solution(mesh):
    return jax.shard_map(
        shards,
        mesh=mesh,
        in_specs=(
            P("col", "row"),
            P("col", "row"),
            P("row", "col"),
            P("row", "col"),
            P("row", "col"),
            P("col", "row"),
            P("col", "row"),
        ),
        out_specs=(P("col", "row"), P("row", "col"), P("col", "row"), P("col", "row")),
        check_vma=False,
    )
```

```python
import jax
import jax.numpy as jnp
from jax import lax
from jax.experimental import pallas as pl
from jax.experimental.pallas import tpu as pltpu
from jax.sharding import PartitionSpec as P

BF = jnp.bfloat16
F32 = jnp.float32
MESH = pl.DeviceIdType.MESH
N_GROUPS = 7
N_ARRIVALS = 60
WIDE = 512
PARTS = 2
RT = 32 // PARTS
VMEM_ALL = 64 * 1024 * 1024 - 65536


def rounded(value):
    return value.astype(BF)


def dot(left, right, dims):
    return lax.dot_general(left, right, (dims, ((), ())), preferred_element_type=F32)


NN = ((1,), (0,))
NT = ((1,), (1,))
TN = ((0,), (0,))


def kernel(
    og_in, li_in, gp_in, up_in, wd_in, wg_in, wu_in,
    ig_out, dg_out, gg_out, ug_out,
    grads, inputs, hidden, backs, backs_sib,
    gp, up, pre, wd_raw, wg_raw, wu_raw, wd, wg, wu,
    part, part_bf, far_lo, far_hi, from_lo, from_hi, z_send, z_recv,
    iq, iq_bf, i_recv, iz_send, iz_recv,
    gg, ug, dg, ig,
    local_sem, send_sem, recv_sem,
):
    units = gp_in.shape[1]
    feats = og_in.shape[2]
    row, col = lax.axis_index("row"), lax.axis_index("col")
    x, zl = lax.div(row, 4), lax.rem(row, 4)
    y, zh, core = lax.div(col, 8), lax.rem(lax.div(col, 2), 4), lax.rem(col, 2)
    sib = 1 - core

    def on(value, step):
        return lax.rem(value + step + 4, 4)

    xp, xm, xo = on(x, 1), on(x, -1), on(x, 2)
    yp, ym, yo = on(y, 1), on(y, -1), on(y, 2)
    hp, hm, ho = on(zh, 1), on(zh, -1), on(zh, 2)

    def at(a, b):
        return a * 4 + b

    X_UP, X_DN, X_OP = [(at(a, zl), col) for a in (xp, xm, xo)]
    Y_UP, Y_DN, Y_OP = [(row, at(a, zh) * 2 + core) for a in (yp, ym, yo)]
    H_UP, H_DN, H_OP = [(row, at(y, b) * 2 + core) for b in (hp, hm, ho)]
    L_TO = [(at(x, on(zl, d)), col) for d in (1, 2, 3)]
    SIB = (row, at(y, zh) * 2 + sib)

    locals_ = []

    def local(src, dst):
        copy = pltpu.make_async_copy(src, dst, local_sem.at[len(locals_)])
        locals_.append(copy)
        copy.start()
        return copy

    arrivals = []

    def arrival():
        arrivals.append(recv_sem.at[len(arrivals)])
        return arrivals[-1]

    def remote(src, dst, where, group, arrived):
        return pltpu.make_async_remote_copy(
            src_ref=src,
            dst_ref=dst,
            send_sem=send_sem.at[group],
            recv_sem=arrived,
            device_id=where,
            device_id_type=MESH,
        )

    def send(src, dst, where, group, arrived):
        remote(src, dst, where, group, arrived).start()

    def same(ref, where, group, arrived):
        remote(ref, ref, where, group, arrived).start()

    def wait(arrived, like):
        remote(like, like, SIB, 0, arrived).wait_recv()

    def wait_sent(group, like):
        remote(like, like, SIB, group, arrivals[0]).wait_send()

    OUT_A, OUT_W, OUT_H, OUT_B, OUT_C, OUT_S, OUT_D = range(N_GROUPS)

    own = at(y, zh)
    c_og = local(og_in, grads.at[core, :, own])
    c_wd = local(wd_in, wd_raw)
    c_gp = local(gp_in, gp)
    c_up = local(up_in, up)
    c_wg = local(wg_in, wg_raw)
    c_wu = local(wu_in, wu_raw)
    c_li = local(li_in, inputs.at[core, :, own])

    barrier = pltpu.get_barrier_semaphore()
    partners = [X_UP, X_DN, X_OP, Y_UP, Y_DN, Y_OP, H_UP, H_DN, H_OP, SIB] + L_TO
    for where in partners:
        pl.semaphore_signal(barrier, inc=1, device_id=where, device_id_type=MESH)
    pl.semaphore_wait(barrier, len(partners))

    def g(block):
        return grads.at[core, :, block]

    def gt(t, block):
        return grads.at[core, t, block]

    TO_H = ((ho, H_OP), (hm, H_UP), (hp, H_DN))
    TO_Y = (Y_OP, Y_UP, Y_DN)
    g_z = [[arrival() for _ in range(3)] for _ in range(PARTS)]
    g_own = arrival()
    for t in range(PARTS):
        for k in range(3):
            send(og_in.at[t], gt(t, own), TO_H[k][1], OUT_A, g_z[t][k])
    for where in TO_Y:
        send(og_in, g(own), where, OUT_A, g_own)

    def padded(raw, ref, copy):
        copy.wait()
        ref[core, 0:units, :] = raw[...]
        ref[core, units:WIDE, :] = jnp.zeros((WIDE - units, feats), BF)
        arrived = arrival()
        same(ref.at[core], SIB, OUT_W, arrived)
        return arrived

    s_wd = padded(wd_raw, wd, c_wd)
    c_gp.wait()
    c_up.wait()
    pre[core] = jnp.zeros((2, 2, 32, WIDE), BF)
    for half in (0, 1):
        pre[core, half, 0, :, 0:units] = gp[half * 32 : half * 32 + 32, :]
        pre[core, half, 1, :, 0:units] = up[half * 32 : half * 32 + 32, :]
    s_pre = arrival()
    same(pre.at[core, sib], SIB, OUT_H, s_pre)
    for half in (0, 1):
        gate = pre[core, half, 0].astype(F32)
        value = rounded(gate * jax.nn.sigmoid(gate) * pre[core, half, 1].astype(F32))
        hidden[half, :, row] = value.reshape(PARTS, RT, WIDE)

    def h(block):
        return hidden.at[:, :, block]

    h_x, h_z = arrival(), arrival()
    for where in (X_OP, X_UP, X_DN):
        same(h(row), where, OUT_H, h_x)

    g_y = [arrival() for _ in range(PARTS)]
    for t in range(PARTS):
        for k in (1, 2, 0):
            block = gt(t, at(y, TO_H[k][0]))
            wait(g_z[t][k], block)
            for where in TO_Y:
                same(block, where, OUT_A, g_y[t])

    def li(block):
        return inputs.at[core, :, block]

    i_z = arrival()
    for _, where in TO_H:
        send(li_in, li(own), where, OUT_A, i_z)

    def partial(t, j):
        rows = grads[core, t].reshape(16 * RT, feats)
        out = dot(rows, wd[j], NT).reshape(16, RT, WIDE)
        part[t * 2 + j] = out
        part_bf[t * 2 + j] = rounded(out)

    def two(ref, u, a, b):
        return ref.at[u, pl.ds(a * 4 + b, 2)]

    n_units = 2 * PARTS
    r_up = [arrival() for _ in range(n_units)]
    r_dn = [arrival() for _ in range(n_units)]
    x_in = [arrival() for _ in range(n_units)]
    z_in = [arrival() for _ in range(n_units)]

    def begin(u):
        send(two(part_bf, u, xo, 0), far_lo.at[u], X_UP, OUT_B, r_up[u])
        send(two(part_bf, u, xo, 2), far_hi.at[u], X_DN, OUT_B, r_dn[u])
        send(two(part_bf, u, xp, 2), from_lo.at[u, pl.ds(2, 2)], X_UP, OUT_B, x_in[u])
        send(two(part_bf, u, xm, 0), from_hi.at[u, pl.ds(0, 2)], X_DN, OUT_B, x_in[u])

    def late(u):
        wait(r_up[u], far_lo.at[u])
        lo = pl.ds(xp * 4, 2)
        part_bf[u, lo] = rounded(part[u, lo] + far_lo[u].astype(F32))
        send(two(part_bf, u, xp, 0), from_lo.at[u, pl.ds(0, 2)], X_UP, OUT_B, x_in[u])
        wait(r_dn[u], far_hi.at[u])
        hi = pl.ds(xm * 4 + 2, 2)
        part_bf[u, hi] = rounded(part[u, hi] + far_hi[u].astype(F32))
        send(two(part_bf, u, xm, 2), from_hi.at[u, pl.ds(2, 2)], X_DN, OUT_B, x_in[u])

    def x_sum(u, b):
        return part[u, at(x, b)] + from_lo[u, b].astype(F32) + from_hi[u, b].astype(F32)

    def along_z(u):
        wait(x_in[u], part_bf.at[u, pl.ds(0, 8)])
        for d in (2, 1, 3):
            z_send[u, d - 1] = rounded(x_sum(u, on(zl, d)))
            send(z_send.at[u, d - 1], z_recv.at[u, d - 1], L_TO[d - 1], OUT_B, z_in[u])

    c_og.wait()
    wait(s_wd, wd.at[sib])
    wait(g_own, grads.at[0, :, pl.ds(0, 3)])
    wait(g_y[0], grads.at[0, 0, pl.ds(0, 9)])
    partial(0, 0)
    begin(0)
    partial(0, 1)
    begin(1)
    late(0)
    wait(g_y[1], grads.at[0, 0, pl.ds(0, 9)])
    partial(1, 0)
    begin(2)
    late(1)
    partial(1, 1)
    begin(3)
    along_z(0)
    late(2)
    along_z(1)
    late(3)
    s_g = arrival()
    same(grads.at[core], SIB, OUT_W, s_g)
    s_wg = padded(wg_raw, wg, c_wg)
    s_wu = padded(wu_raw, wu, c_wu)
    along_z(2)

    along_z(3)
    wait(s_pre, pre.at[sib, core])

    def b_ref(t, a, b):
        return backs.at[t, at(a, b)]

    b_z = [[arrival() for _ in range(3)] for _ in range(PARTS)]
    b_one = [[arrival() for _ in range(4)] for _ in range(PARTS)]
    b_up = [arrival() for _ in range(PARTS)]
    b_dn = [arrival() for _ in range(PARTS)]
    b_far = [arrival() for _ in range(PARTS)]

    def start_backs(t):
        for j in (0, 1):
            u = t * 2 + j
            wait(z_in[u], z_recv.at[u])
            back = x_sum(u, zl)
            for d in (1, 2, 3):
                back = back + z_recv[u, d - 1].astype(F32)
            rows = pl.ds(t * RT, RT)
            gate = pre[j, core, 0, rows].astype(F32)
            upper = pre[j, core, 1, rows].astype(F32)
            sig = jax.nn.sigmoid(gate)
            backs[t, row, 0, j] = rounded(back * upper * sig * (1.0 + gate * (1.0 - sig)))
            backs[t, row, 1, j] = rounded(back * gate * sig)
        for d in (2, 1, 3):
            same(backs.at[t, row], L_TO[d - 1], OUT_C, b_z[t][d - 1])
        same(backs.at[t, row], X_OP, OUT_C, b_far[t])
        same(backs.at[t, row], X_UP, OUT_C, b_up[t])
        same(backs.at[t, row], X_DN, OUT_C, b_dn[t])

    start_backs(0)

    wait(i_z, inputs.at[0, :, pl.ds(0, 3)])
    c_li.wait()
    i_y = arrival()
    for where in TO_Y:
        same(inputs.at[core, :, pl.ds(y * 4, 4)], where, OUT_H, i_y)
    start_backs(1)

    def from_z(t, d):
        ref = b_ref(t, x, on(zl, -d))
        wait(b_z[t][d - 1], ref)
        if d != 1:
            same(ref, X_UP, OUT_C, b_one[t][0 if d == 2 else 1])
        if d != 2:
            same(ref, X_DN, OUT_C, b_one[t][2 if d == 1 else 3])

    def last_x(t):
        same(b_ref(t, x, on(zl, -1)), X_UP, OUT_C, b_up[t])
        same(b_ref(t, x, on(zl, -2)), X_DN, OUT_C, b_dn[t])

    def forward(t, d):
        up_ref, dn_ref = b_ref(t, xm, on(zl, -d)), b_ref(t, xp, on(zl, -d))
        if d == 2:
            wait(b_one[t][0], up_ref)
            same(up_ref, X_UP, OUT_C, b_far[t])
        elif d == 1:
            wait(b_one[t][2], dn_ref)
            same(dn_ref, X_DN, OUT_C, b_far[t])
        else:
            wait(b_one[t][1], up_ref)
            same(up_ref.at[0], X_UP, OUT_C, b_far[t])
            wait(b_one[t][3], dn_ref)
            same(dn_ref.at[1], X_DN, OUT_C, b_far[t])

    s_b = arrival()
    q_y = [arrival() for _ in range(PARTS)]
    q_z = [arrival() for _ in range(PARTS)]

    def to_y(t, a):
        @pl.when(a != y)
        def _():
            where = (row, at(a, zh) * 2 + core)
            send(iq_bf.at[t, pl.ds(a * 4, 4)], i_recv.at[t, y], where, OUT_D, q_y[t])

    def use(t, planes):
        total = None
        for k, weight in ((0, wg), (1, wu)):
            for j in (0, 1):
                rows = [backs[t, pl.ds(a * 4, 4), k, j].reshape(4 * RT, WIDE) for a in planes]
                rows = rows[0] if len(rows) == 1 else jnp.concatenate(rows, axis=0)
                term = dot(rows, weight[j], NN)
                total = term if total is None else total + term
        for k, a in enumerate(planes):
            out = total[k * 4 * RT : (k + 1) * 4 * RT].reshape(4, RT, feats)
            some = pl.ds(a * 4, 4)
            iq[t, some] = out
            iq_bf[t, some] = rounded(out)
            to_y(t, a)
            send(backs.at[t, some, :, sib], backs_sib.at[t, some], SIB, OUT_S, s_b)

    def y_sum(t, b):
        out = iq[t, at(y, b)]
        for k in range(3):
            out = out + i_recv[t, on(y, k + 1), b].astype(F32)
        return out

    def along_h(t):
        wait(q_y[t], i_recv.at[t, pl.ds(0, 3)])
        for k, (b, where) in enumerate(((ho, H_OP), (hp, H_UP), (hm, H_DN))):
            iz_send[t, k] = rounded(y_sum(t, b))
            send(iz_send.at[t, k], iz_recv.at[t, k], where, OUT_D, q_z[t])

    def finish(t):
        wait(q_z[t], iz_recv.at[t])
        total = y_sum(t, zh)
        for k in range(3):
            total = total + iz_recv[t, k].astype(F32)
        ig[t] = rounded(total)

    from_z(0, 2)
    from_z(0, 1)
    from_z(0, 3)
    last_x(0)
    forward(0, 2)
    forward(0, 1)
    from_z(1, 2)
    from_z(1, 1)
    from_z(1, 3)
    forward(0, 3)
    last_x(1)

    for where in L_TO:
        same(h(row), where, OUT_H, h_z)
    wait(s_wg, wg.at[sib])
    wait(s_wu, wu.at[sib])
    forward(1, 2)
    wait(b_up[0], backs.at[0, pl.ds(0, 2)])
    wait(b_dn[0], backs.at[0, pl.ds(0, 2)])
    use(0, (x, xm, xp))
    forward(1, 1)
    forward(1, 3)
    wait(b_far[0], backs.at[0, pl.ds(0, 4)])
    use(0, (xo,))
    wait(i_y, inputs.at[0, :, pl.ds(0, 12)])
    s_i = arrival()
    same(inputs.at[core], SIB, OUT_H, s_i)

    wait(b_up[1], backs.at[1, pl.ds(0, 2)])
    wait(b_dn[1], backs.at[1, pl.ds(0, 2)])
    use(1, (x, xm, xp))

    def hidden_x():
        wait(h_z, hidden.at[:, :, pl.ds(0, 3)])
        for d in (1, 2, 3):
            for where in (X_OP, X_UP, X_DN):
                same(h(at(x, on(zl, -d))), where, OUT_H, h_x)

    pl.when(core == 0)(hidden_x)
    along_h(0)
    wait(b_far[1], backs.at[1, pl.ds(0, 4)])
    use(1, (xo,))
    along_h(1)
    pl.when(core == 1)(hidden_x)

    def tokens(value):
        return value.reshape(512, value.shape[-1])

    wait(s_i, inputs.at[sib])
    wait(s_b, backs_sib)
    outs = []
    for k, ref, out in ((0, gg, gg_out), (1, ug, ug_out)):
        value = dot(tokens(backs[:, :, k, core]), tokens(inputs[core]), TN)
        value = value + dot(tokens(backs_sib[:, :, k]), tokens(inputs[sib]), TN)
        ref[...] = rounded(value[0:units, :])
        outs.append(local(ref, out))
    finish(0)
    wait(h_x, hidden.at[:, :, pl.ds(0, 12)])
    wait(s_g, grads.at[sib])
    dg[...] = rounded(
        dot(hidden[...].reshape(1024, WIDE), grads[...].reshape(1024, feats), TN)[0:units, :]
    )
    outs.append(local(dg, dg_out))
    finish(1)
    outs.append(local(ig, ig_out))

    wait_sent(OUT_A, grads.at[:, :, pl.ds(0, 9)])
    wait_sent(OUT_W, backs)
    wait_sent(OUT_H, backs.at[:, pl.ds(0, 15)])
    wait_sent(OUT_B, grads.at[:, :, pl.ds(0, 15)])
    wait_sent(OUT_C, backs.at[:, pl.ds(0, 15)])
    wait_sent(OUT_S, backs.at[0])
    wait_sent(OUT_D, grads.at[0, :, pl.ds(0, 15)])
    for copy in outs:
        copy.wait()
    assert len(arrivals) == N_ARRIVALS, len(arrivals)


def hand_over(*refs):
    sources, targets, rooms, sem = refs[:4], refs[4:8], refs[8:12], refs[12]
    into = [pltpu.make_async_copy(s, v, sem.at[k]) for k, (s, v) in enumerate(zip(sources, rooms))]
    out = [pltpu.make_async_copy(v, t, sem.at[4 + k]) for k, (v, t) in enumerate(zip(rooms, targets))]
    for copy in into:
        copy.start()
    for first, second in zip(into, out):
        first.wait()
        second.start()
    for copy in out:
        copy.wait()


def shards(out_grad, layer_input, gate_preact, up_preact, w_down, w_gate, w_up):
    tokens, feats = out_grad.shape
    units = gate_preact.shape[1]
    vm = pltpu.VMEM
    any_space = pl.BlockSpec(memory_space=pl.ANY)
    shapes = (
        jax.ShapeDtypeStruct((PARTS, RT, feats), BF),
        jax.ShapeDtypeStruct((units, feats), BF),
        jax.ShapeDtypeStruct((units, feats), BF),
        jax.ShapeDtypeStruct((units, feats), BF),
    )
    results = pl.pallas_call(
        kernel,
        out_shape=shapes,
        in_specs=[any_space] * 7,
        out_specs=(any_space,) * 4,
        scratch_shapes=[
            vm((2, PARTS, 16, RT, feats), BF),
            vm((2, PARTS, 16, RT, feats), BF),
            vm((2, PARTS, 16, RT, WIDE), BF),
            vm((PARTS, 16, 2, 2, RT, WIDE), BF),
            vm((PARTS, 16, 2, RT, WIDE), BF),
            vm((64, units), BF), vm((64, units), BF), vm((2, 2, 2, 32, WIDE), BF),
            vm((units, feats), BF), vm((units, feats), BF), vm((units, feats), BF),
            vm((2, WIDE, feats), BF), vm((2, WIDE, feats), BF), vm((2, WIDE, feats), BF),
            vm((2 * PARTS, 16, RT, WIDE), F32), vm((2 * PARTS, 16, RT, WIDE), BF),
            vm((2 * PARTS, 2, RT, WIDE), BF), vm((2 * PARTS, 2, RT, WIDE), BF),
            vm((2 * PARTS, 4, RT, WIDE), BF), vm((2 * PARTS, 4, RT, WIDE), BF),
            vm((2 * PARTS, 3, RT, WIDE), BF), vm((2 * PARTS, 3, RT, WIDE), BF),
            vm((PARTS, 16, RT, feats), F32), vm((PARTS, 16, RT, feats), BF),
            vm((PARTS, 4, 4, RT, feats), BF),
            vm((PARTS, 3, RT, feats), BF), vm((PARTS, 3, RT, feats), BF),
            vm((units, feats), BF), vm((units, feats), BF), vm((units, feats), BF),
            vm((PARTS, RT, feats), BF),
            pltpu.SemaphoreType.DMA((11,)),
            pltpu.SemaphoreType.DMA((N_GROUPS,)),
            pltpu.SemaphoreType.DMA((N_ARRIVALS,)),
        ],
        compiler_params=pltpu.CompilerParams(
            collective_id=0, has_side_effects=True, vmem_limit_bytes=VMEM_ALL
        ),
        cost_estimate=pl.CostEstimate(
            flops=12 * 1024 * units * feats, bytes_accessed=3_000_000, transcendentals=64 * units
        ),
        name="swiglu_back",
    )(
        out_grad.reshape(PARTS, RT, feats),
        layer_input.reshape(PARTS, RT, feats),
        gate_preact,
        up_preact,
        w_down.T,
        w_gate,
        w_up,
    )
    ig, dg, gg, ug = pl.pallas_call(
        hand_over,
        out_shape=shapes,
        in_specs=[any_space] * 4,
        out_specs=(any_space,) * 4,
        scratch_shapes=[vm(s.shape, s.dtype) for s in shapes] + [pltpu.SemaphoreType.DMA((8,))],
        compiler_params=pltpu.CompilerParams(vmem_limit_bytes=VMEM_ALL),
        name="hand_over",
    )(*results)
    return ig.reshape(tokens, feats), dg.T, gg, ug


def solution(mesh):
    return jax.shard_map(
        shards,
        mesh=mesh,
        in_specs=(
            P("col", "row"),
            P("col", "row"),
            P("row", "col"),
            P("row", "col"),
            P("row", "col"),
            P("col", "row"),
            P("col", "row"),
        ),
        out_specs=(P("col", "row"), P("row", "col"), P("col", "row"), P("col", "row")),
        check_vma=False,
    )
```

```python
import jax
import jax.numpy as jnp
from jax import lax
from jax.experimental import pallas as pl
from jax.experimental.pallas import tpu as pltpu
from jax.sharding import PartitionSpec as P

BF = jnp.bfloat16
F32 = jnp.float32
MESH = pl.DeviceIdType.MESH
N_GROUPS = 7
N_ARRIVALS = 56
WIDE = 512
PARTS = 2
RT = 32 // PARTS
VMEM_ALL = 64 * 1024 * 1024 - 65536


def rounded(value):
    return value.astype(BF)


def dot(left, right, dims):
    return lax.dot_general(left, right, (dims, ((), ())), preferred_element_type=F32)


NN = ((1,), (0,))
NT = ((1,), (1,))
TN = ((0,), (0,))


def kernel(
    og_in, li_in, gp_in, up_in, wd_in, wg_in, wu_in,
    ig_out, dg_out, gg_out, ug_out,
    grads, inputs, hidden, backs, backs_sib,
    gp, up, pre, wd_raw, wg_raw, wu_raw, wd, wg, wu,
    part, part_bf, x_recv, z_send, z_recv,
    iq, iq_bf, i_recv, iz_send, iz_recv,
    gg, ug, dg, ig,
    local_sem, send_sem, recv_sem,
):
    units = gp_in.shape[1]
    feats = og_in.shape[2]
    row, col = lax.axis_index("row"), lax.axis_index("col")
    x, zl = lax.div(row, 4), lax.rem(row, 4)
    y, zh, core = lax.div(col, 8), lax.rem(lax.div(col, 2), 4), lax.rem(col, 2)
    sib = 1 - core

    def on(value, step):
        return lax.rem(value + step + 4, 4)

    xp, xm, xo = on(x, 1), on(x, -1), on(x, 2)
    yp, ym, yo = on(y, 1), on(y, -1), on(y, 2)
    hp, hm, ho = on(zh, 1), on(zh, -1), on(zh, 2)

    def at(a, b):
        return a * 4 + b

    X_UP, X_DN, X_OP = [(at(a, zl), col) for a in (xp, xm, xo)]
    Y_UP, Y_DN, Y_OP = [(row, at(a, zh) * 2 + core) for a in (yp, ym, yo)]
    H_UP, H_DN, H_OP = [(row, at(y, b) * 2 + core) for b in (hp, hm, ho)]
    L_TO = [(at(x, on(zl, d)), col) for d in (1, 2, 3)]
    SIB = (row, at(y, zh) * 2 + sib)

    locals_ = []

    def local(src, dst):
        copy = pltpu.make_async_copy(src, dst, local_sem.at[len(locals_)])
        locals_.append(copy)
        copy.start()
        return copy

    arrivals = []

    def arrival():
        arrivals.append(recv_sem.at[len(arrivals)])
        return arrivals[-1]

    def remote(src, dst, where, group, arrived):
        return pltpu.make_async_remote_copy(
            src_ref=src,
            dst_ref=dst,
            send_sem=send_sem.at[group],
            recv_sem=arrived,
            device_id=where,
            device_id_type=MESH,
        )

    def send(src, dst, where, group, arrived):
        remote(src, dst, where, group, arrived).start()

    def same(ref, where, group, arrived):
        remote(ref, ref, where, group, arrived).start()

    def wait(arrived, like):
        remote(like, like, SIB, 0, arrived).wait_recv()

    def wait_sent(group, like):
        remote(like, like, SIB, group, arrivals[0]).wait_send()

    OUT_A, OUT_W, OUT_H, OUT_B, OUT_C, OUT_S, OUT_D = range(N_GROUPS)

    own = at(y, zh)
    c_og = local(og_in, grads.at[core, :, own])
    c_wd = local(wd_in, wd_raw)
    c_gp = local(gp_in, gp)
    c_up = local(up_in, up)
    c_wg = local(wg_in, wg_raw)
    c_wu = local(wu_in, wu_raw)
    c_li = local(li_in, inputs.at[core, :, own])

    barrier = pltpu.get_barrier_semaphore()
    partners = [X_UP, X_DN, X_OP, Y_UP, Y_DN, Y_OP, H_UP, H_DN, SIB] + L_TO
    for where in partners:
        pl.semaphore_signal(barrier, inc=1, device_id=where, device_id_type=MESH)
    pl.semaphore_wait(barrier, len(partners))

    def g(block):
        return grads.at[core, :, block]

    def gt(t, block):
        return grads.at[core, t, block]

    TO_H = ((ho, H_OP), (hm, H_UP), (hp, H_DN))
    TO_Y = (Y_OP, Y_UP, Y_DN)
    g_z = [[arrival() for _ in range(3)] for _ in range(PARTS)]
    g_own = arrival()
    for t, k in ((0, 1), (1, 2), (1, 1), (0, 2)):
        send(og_in.at[t], gt(t, own), TO_H[k][1], OUT_A, g_z[t][k])
    for where in TO_Y:
        send(og_in, g(own), where, OUT_A, g_own)

    def padded(raw, ref, copy):
        copy.wait()
        ref[core, 0:units, :] = raw[...]
        ref[core, units:WIDE, :] = jnp.zeros((WIDE - units, feats), BF)
        arrived = arrival()
        same(ref.at[core], SIB, OUT_W, arrived)
        return arrived

    s_wd = padded(wd_raw, wd, c_wd)
    c_gp.wait()
    c_up.wait()
    pre[core] = jnp.zeros((2, 2, 32, WIDE), BF)
    for half in (0, 1):
        pre[core, half, 0, :, 0:units] = gp[half * 32 : half * 32 + 32, :]
        pre[core, half, 1, :, 0:units] = up[half * 32 : half * 32 + 32, :]
    s_pre = arrival()
    same(pre.at[core, sib], SIB, OUT_H, s_pre)
    for half in (0, 1):
        gate = pre[core, half, 0].astype(F32)
        value = rounded(gate * jax.nn.sigmoid(gate) * pre[core, half, 1].astype(F32))
        hidden[half, :, row] = value.reshape(PARTS, RT, WIDE)

    def h(block):
        return hidden.at[:, :, block]

    h_x, h_z = arrival(), arrival()
    h_one = [arrival() for _ in range(4)]
    for where in (X_OP, X_UP, X_DN):
        same(h(row), where, OUT_H, h_x)

    g_y = [arrival() for _ in range(PARTS)]
    def g_from_z(t, k):
        block = gt(t, at(y, TO_H[k][0]))
        wait(g_z[t][k], block)
        if (t, k) in ((0, 1), (1, 2)):
            same(block, TO_H[k][1], OUT_A, g_z[t][0])
        for where in TO_Y:
            same(block, where, OUT_A, g_y[t])

    for t, k in ((0, 1), (1, 2), (0, 2), (1, 1), (0, 0), (1, 0)):
        g_from_z(t, k)

    def li(block):
        return inputs.at[core, :, block]

    i_z = arrival()
    for _, where in TO_H:
        send(li_in, li(own), where, OUT_A, i_z)

    def partial(t, j):
        rows = grads[core, t].reshape(16 * RT, feats)
        out = dot(rows, wd[j], NT).reshape(16, RT, WIDE)
        part[t * 2 + j] = out
        part_bf[t * 2 + j] = rounded(out)

    n_units = 2 * PARTS
    x_in = [arrival() for _ in range(n_units)]
    z_in = [arrival() for _ in range(n_units)]

    def begin(u):
        for k, (a, where) in enumerate(((xo, X_OP), (xp, X_UP), (xm, X_DN))):
            send(part_bf.at[u, pl.ds(a * 4, 4)], x_recv.at[u, k], where, OUT_B, x_in[u])

    def x_sum(u, b):
        out = part[u, at(x, b)]
        for k in range(3):
            out = out + x_recv[u, k, b].astype(F32)
        return out

    def along_z(u):
        wait(x_in[u], x_recv.at[u])
        for d in (2, 1, 3):
            z_send[u, d - 1] = rounded(x_sum(u, on(zl, d)))
            send(z_send.at[u, d - 1], z_recv.at[u, d - 1], L_TO[d - 1], OUT_B, z_in[u])

    c_og.wait()
    wait(s_wd, wd.at[sib])
    wait(g_own, grads.at[0, :, pl.ds(0, 3)])
    wait(g_y[0], grads.at[0, 0, pl.ds(0, 9)])
    partial(0, 0)
    begin(0)
    partial(0, 1)
    begin(1)
    wait(g_y[1], grads.at[0, 0, pl.ds(0, 9)])
    partial(1, 0)
    begin(2)
    partial(1, 1)
    begin(3)
    along_z(0)
    along_z(1)
    s_g = arrival()
    same(grads.at[core], SIB, OUT_W, s_g)
    s_wg = padded(wg_raw, wg, c_wg)
    s_wu = padded(wu_raw, wu, c_wu)
    along_z(2)

    along_z(3)
    wait(s_pre, pre.at[sib, core])

    def b_ref(t, a, b):
        return backs.at[t, at(a, b)]

    b_z = [[arrival() for _ in range(3)] for _ in range(PARTS)]
    b_one = [[arrival() for _ in range(4)] for _ in range(PARTS)]
    b_up = [arrival() for _ in range(PARTS)]
    b_dn = [arrival() for _ in range(PARTS)]
    b_far = [arrival() for _ in range(PARTS)]

    def start_backs(t):
        for j in (0, 1):
            u = t * 2 + j
            wait(z_in[u], z_recv.at[u])
            back = x_sum(u, zl)
            for d in (1, 2, 3):
                back = back + z_recv[u, d - 1].astype(F32)
            rows = pl.ds(t * RT, RT)
            gate = pre[j, core, 0, rows].astype(F32)
            upper = pre[j, core, 1, rows].astype(F32)
            sig = jax.nn.sigmoid(gate)
            backs[t, row, 0, j] = rounded(back * upper * sig * (1.0 + gate * (1.0 - sig)))
            backs[t, row, 1, j] = rounded(back * gate * sig)
        for d in (2, 1, 3):
            same(backs.at[t, row], L_TO[d - 1], OUT_C, b_z[t][d - 1])
        same(backs.at[t, row], X_OP, OUT_C, b_far[t])
        same(backs.at[t, row], X_UP, OUT_C, b_up[t])
        same(backs.at[t, row], X_DN, OUT_C, b_dn[t])

    start_backs(0)

    wait(i_z, inputs.at[0, :, pl.ds(0, 3)])
    c_li.wait()
    i_y = arrival()
    for where in TO_Y:
        same(inputs.at[core, :, pl.ds(y * 4, 4)], where, OUT_H, i_y)
    start_backs(1)

    def from_z(t, d):
        ref = b_ref(t, x, on(zl, -d))
        wait(b_z[t][d - 1], ref)
        if d != 1:
            same(ref, X_UP, OUT_C, b_one[t][0 if d == 2 else 1])
        if d != 2:
            same(ref, X_DN, OUT_C, b_one[t][2 if d == 1 else 3])

    def last_x(t):
        same(b_ref(t, x, on(zl, -1)), X_UP, OUT_C, b_up[t])
        same(b_ref(t, x, on(zl, -2)), X_DN, OUT_C, b_dn[t])

    def forward(t, d):
        up_ref, dn_ref = b_ref(t, xm, on(zl, -d)), b_ref(t, xp, on(zl, -d))
        if d == 2:
            wait(b_one[t][0], up_ref)
            same(up_ref, X_UP, OUT_C, b_far[t])
        elif d == 1:
            wait(b_one[t][2], dn_ref)
            same(dn_ref, X_DN, OUT_C, b_far[t])
        else:
            wait(b_one[t][1], up_ref)
            same(up_ref.at[0], X_UP, OUT_C, b_far[t])
            wait(b_one[t][3], dn_ref)
            same(dn_ref.at[1], X_DN, OUT_C, b_far[t])

    s_b = arrival()
    q_y = [arrival() for _ in range(PARTS)]
    q_z = [arrival() for _ in range(PARTS)]

    def to_y(t, a):
        @pl.when(a != y)
        def _():
            where = (row, at(a, zh) * 2 + core)
            send(iq_bf.at[t, pl.ds(a * 4, 4)], i_recv.at[t, y], where, OUT_D, q_y[t])

    def use(t, planes):
        total = None
        for k, weight in ((0, wg), (1, wu)):
            for j in (0, 1):
                rows = [backs[t, pl.ds(a * 4, 4), k, j].reshape(4 * RT, WIDE) for a in planes]
                rows = rows[0] if len(rows) == 1 else jnp.concatenate(rows, axis=0)
                term = dot(rows, weight[j], NN)
                total = term if total is None else total + term
        for k, a in enumerate(planes):
            out = total[k * 4 * RT : (k + 1) * 4 * RT].reshape(4, RT, feats)
            some = pl.ds(a * 4, 4)
            iq[t, some] = out
            iq_bf[t, some] = rounded(out)
            to_y(t, a)
            send(backs.at[t, some, :, sib], backs_sib.at[t, some], SIB, OUT_S, s_b)

    def y_sum(t, b):
        out = iq[t, at(y, b)]
        for k in range(3):
            out = out + i_recv[t, on(y, k + 1), b].astype(F32)
        return out

    def along_h(t):
        wait(q_y[t], i_recv.at[t, pl.ds(0, 3)])
        for k, (b, where) in enumerate(((ho, H_OP), (hp, H_UP), (hm, H_DN))):
            iz_send[t, k] = rounded(y_sum(t, b))
            send(iz_send.at[t, k], iz_recv.at[t, k], where, OUT_D, q_z[t])

    def finish(t):
        wait(q_z[t], iz_recv.at[t])
        total = y_sum(t, zh)
        for k in range(3):
            total = total + iz_recv[t, k].astype(F32)
        ig[t] = rounded(total)

    from_z(0, 2)
    from_z(0, 1)
    from_z(0, 3)
    last_x(0)
    forward(0, 2)
    forward(0, 1)
    from_z(1, 2)
    from_z(1, 1)
    from_z(1, 3)
    forward(0, 3)
    last_x(1)

    for where in L_TO:
        same(h(row), where, OUT_H, h_z)
    wait(s_wg, wg.at[sib])
    wait(s_wu, wu.at[sib])
    forward(1, 2)
    wait(b_up[0], backs.at[0, pl.ds(0, 2)])
    wait(b_dn[0], backs.at[0, pl.ds(0, 2)])
    use(0, (x, xm, xp))
    forward(1, 1)
    forward(1, 3)
    wait(b_far[0], backs.at[0, pl.ds(0, 4)])
    use(0, (xo,))
    wait(i_y, inputs.at[0, :, pl.ds(0, 12)])
    s_i = arrival()
    same(inputs.at[core], SIB, OUT_H, s_i)

    wait(b_up[1], backs.at[1, pl.ds(0, 2)])
    wait(b_dn[1], backs.at[1, pl.ds(0, 2)])
    use(1, (x, xm, xp))

    def hidden_x():
        wait(h_z, hidden.at[:, :, pl.ds(0, 3)])
        one, two, three = [h(at(x, on(zl, -d))) for d in (1, 2, 3)]
        same(two, X_UP, OUT_H, h_one[0])
        same(one, X_DN, OUT_H, h_one[2])
        same(three, X_UP, OUT_H, h_one[1])
        same(three, X_DN, OUT_H, h_one[3])
        same(one, X_UP, OUT_H, h_x)
        same(two, X_DN, OUT_H, h_x)

    def hidden_forward():
        ref = h(at(xm, on(zl, -2)))
        wait(h_one[0], ref)
        same(ref, X_UP, OUT_H, h_x)
        ref = h(at(xp, on(zl, -1)))
        wait(h_one[2], ref)
        same(ref, X_DN, OUT_H, h_x)
        wait(h_one[1], ref)
        same(hidden.at[0, :, at(xm, on(zl, -3))], X_UP, OUT_H, h_x)
        wait(h_one[3], ref)
        same(hidden.at[1, :, at(xp, on(zl, -3))], X_DN, OUT_H, h_x)

    wait(b_far[1], backs.at[1, pl.ds(0, 4)])
    pl.when(core == 0)(hidden_x)
    use(1, (xo,))
    along_h(0)
    along_h(1)

    def tokens(value):
        return value.reshape(512, value.shape[-1])

    wait(s_i, inputs.at[sib])
    pl.when(core == 1)(hidden_x)
    wait(s_b, backs_sib)
    hidden_forward()
    outs = []
    for k, ref, out in ((0, gg, gg_out), (1, ug, ug_out)):
        value = dot(tokens(backs[:, :, k, core]), tokens(inputs[core]), TN)
        value = value + dot(tokens(backs_sib[:, :, k]), tokens(inputs[sib]), TN)
        ref[...] = rounded(value[0:units, :])
        outs.append(local(ref, out))
    finish(0)
    wait(h_x, hidden.at[0])
    wait(s_g, grads.at[sib])
    dg[...] = rounded(
        dot(hidden[...].reshape(1024, WIDE), grads[...].reshape(1024, feats), TN)[0:units, :]
    )
    outs.append(local(dg, dg_out))
    finish(1)
    outs.append(local(ig, ig_out))

    wait_sent(OUT_A, grads.at[:, :, pl.ds(0, 9)])
    wait_sent(OUT_W, backs)
    wait_sent(OUT_H, backs.at[:, pl.ds(0, 15)])
    wait_sent(OUT_B, grads.at[:, :, pl.ds(0, 15)])
    wait_sent(OUT_C, backs.at[:, pl.ds(0, 15)])
    wait_sent(OUT_S, backs.at[0])
    wait_sent(OUT_D, grads.at[0, :, pl.ds(0, 15)])
    for copy in outs:
        copy.wait()
    assert len(arrivals) == N_ARRIVALS, len(arrivals)


def hand_over(*refs):
    sources, targets, rooms, sem = refs[:4], refs[4:8], refs[8:12], refs[12]
    into = [pltpu.make_async_copy(s, v, sem.at[k]) for k, (s, v) in enumerate(zip(sources, rooms))]
    out = [pltpu.make_async_copy(v, t, sem.at[4 + k]) for k, (v, t) in enumerate(zip(rooms, targets))]
    for copy in into:
        copy.start()
    for first, second in zip(into, out):
        first.wait()
        second.start()
    for copy in out:
        copy.wait()


def shards(out_grad, layer_input, gate_preact, up_preact, w_down, w_gate, w_up):
    tokens, feats = out_grad.shape
    units = gate_preact.shape[1]
    vm = pltpu.VMEM
    any_space = pl.BlockSpec(memory_space=pl.ANY)
    shapes = (
        jax.ShapeDtypeStruct((PARTS, RT, feats), BF),
        jax.ShapeDtypeStruct((units, feats), BF),
        jax.ShapeDtypeStruct((units, feats), BF),
        jax.ShapeDtypeStruct((units, feats), BF),
    )
    results = pl.pallas_call(
        kernel,
        out_shape=shapes,
        in_specs=[any_space] * 7,
        out_specs=(any_space,) * 4,
        scratch_shapes=[
            vm((2, PARTS, 16, RT, feats), BF),
            vm((2, PARTS, 16, RT, feats), BF),
            vm((2, PARTS, 16, RT, WIDE), BF),
            vm((PARTS, 16, 2, 2, RT, WIDE), BF),
            vm((PARTS, 16, 2, RT, WIDE), BF),
            vm((64, units), BF), vm((64, units), BF), vm((2, 2, 2, 32, WIDE), BF),
            vm((units, feats), BF), vm((units, feats), BF), vm((units, feats), BF),
            vm((2, WIDE, feats), BF), vm((2, WIDE, feats), BF), vm((2, WIDE, feats), BF),
            vm((2 * PARTS, 16, RT, WIDE), F32), vm((2 * PARTS, 16, RT, WIDE), BF),
            vm((2 * PARTS, 3, 4, RT, WIDE), BF),
            vm((2 * PARTS, 3, RT, WIDE), BF), vm((2 * PARTS, 3, RT, WIDE), BF),
            vm((PARTS, 16, RT, feats), F32), vm((PARTS, 16, RT, feats), BF),
            vm((PARTS, 4, 4, RT, feats), BF),
            vm((PARTS, 3, RT, feats), BF), vm((PARTS, 3, RT, feats), BF),
            vm((units, feats), BF), vm((units, feats), BF), vm((units, feats), BF),
            vm((PARTS, RT, feats), BF),
            pltpu.SemaphoreType.DMA((11,)),
            pltpu.SemaphoreType.DMA((N_GROUPS,)),
            pltpu.SemaphoreType.DMA((N_ARRIVALS,)),
        ],
        compiler_params=pltpu.CompilerParams(
            collective_id=0, has_side_effects=True, vmem_limit_bytes=VMEM_ALL
        ),
        cost_estimate=pl.CostEstimate(
            flops=12 * 1024 * units * feats, bytes_accessed=3_000_000, transcendentals=64 * units
        ),
        name="swiglu_back",
    )(
        out_grad.reshape(PARTS, RT, feats),
        layer_input.reshape(PARTS, RT, feats),
        gate_preact,
        up_preact,
        w_down.T,
        w_gate,
        w_up,
    )
    ig, dg, gg, ug = pl.pallas_call(
        hand_over,
        out_shape=shapes,
        in_specs=[any_space] * 4,
        out_specs=(any_space,) * 4,
        scratch_shapes=[vm(s.shape, s.dtype) for s in shapes] + [pltpu.SemaphoreType.DMA((8,))],
        compiler_params=pltpu.CompilerParams(vmem_limit_bytes=VMEM_ALL),
        name="hand_over",
    )(*results)
    return ig.reshape(tokens, feats), dg.T, gg, ug


def solution(mesh):
    return jax.shard_map(
        shards,
        mesh=mesh,
        in_specs=(
            P("col", "row"),
            P("col", "row"),
            P("row", "col"),
            P("row", "col"),
            P("row", "col"),
            P("col", "row"),
            P("col", "row"),
        ),
        out_specs=(P("col", "row"), P("row", "col"), P("col", "row"), P("col", "row")),
        check_vma=False,
    )
```

```python
import jax
import jax.numpy as jnp
from jax import lax
from jax.experimental import pallas as pl
from jax.experimental.pallas import tpu as pltpu
from jax.sharding import PartitionSpec as P

BF = jnp.bfloat16
F32 = jnp.float32
MESH = pl.DeviceIdType.MESH
N_GROUPS = 7
N_ARRIVALS = 58
WIDE = 512
PARTS = 2
RT = 32 // PARTS
VMEM_ALL = 64 * 1024 * 1024 - 65536


def rounded(value):
    return value.astype(BF)


def dot(left, right, dims):
    return lax.dot_general(left, right, (dims, ((), ())), preferred_element_type=F32)


NN = ((1,), (0,))
NT = ((1,), (1,))
TN = ((0,), (0,))


def kernel(
    og_in, li_in, gp_in, up_in, wd_in, wg_in, wu_in,
    ig_out, dg_out, gg_out, ug_out,
    grads, inputs, hidden, backs, backs_sib,
    gp, up, pre, wd_raw, wg_raw, wu_raw, wd, wg, wu,
    part, part_bf, x_recv, z_send, z_recv,
    iq, iq_bf, i_recv, iz_send, iz_recv,
    gg, ug, dg, ig,
    local_sem, send_sem, recv_sem,
):
    units = gp_in.shape[1]
    feats = og_in.shape[2]
    row, col = lax.axis_index("row"), lax.axis_index("col")
    x, zl = lax.div(row, 4), lax.rem(row, 4)
    y, zh, core = lax.div(col, 8), lax.rem(lax.div(col, 2), 4), lax.rem(col, 2)
    sib = 1 - core

    def on(value, step):
        return lax.rem(value + step + 4, 4)

    xp, xm, xo = on(x, 1), on(x, -1), on(x, 2)
    yp, ym, yo = on(y, 1), on(y, -1), on(y, 2)
    hp, hm, ho = on(zh, 1), on(zh, -1), on(zh, 2)

    def at(a, b):
        return a * 4 + b

    X_UP, X_DN, X_OP = [(at(a, zl), col) for a in (xp, xm, xo)]
    Y_UP, Y_DN, Y_OP = [(row, at(a, zh) * 2 + core) for a in (yp, ym, yo)]
    H_UP, H_DN, H_OP = [(row, at(y, b) * 2 + core) for b in (hp, hm, ho)]
    L_TO = [(at(x, on(zl, d)), col) for d in (1, 2, 3)]
    SIB = (row, at(y, zh) * 2 + sib)

    locals_ = []

    def local(src, dst):
        copy = pltpu.make_async_copy(src, dst, local_sem.at[len(locals_)])
        locals_.append(copy)
        copy.start()
        return copy

    arrivals = []

    def arrival():
        arrivals.append(recv_sem.at[len(arrivals)])
        return arrivals[-1]

    def remote(src, dst, where, group, arrived):
        return pltpu.make_async_remote_copy(
            src_ref=src,
            dst_ref=dst,
            send_sem=send_sem.at[group],
            recv_sem=arrived,
            device_id=where,
            device_id_type=MESH,
        )

    def send(src, dst, where, group, arrived):
        remote(src, dst, where, group, arrived).start()

    def same(ref, where, group, arrived):
        remote(ref, ref, where, group, arrived).start()

    def wait(arrived, like):
        remote(like, like, SIB, 0, arrived).wait_recv()

    def wait_sent(group, like):
        remote(like, like, SIB, group, arrivals[0]).wait_send()

    OUT_A, OUT_W, OUT_H, OUT_B, OUT_C, OUT_S, OUT_D = range(N_GROUPS)

    own = at(y, zh)
    c_og = local(og_in, grads.at[core, :, own])
    c_wd = local(wd_in, wd_raw)
    c_gp = local(gp_in, gp)
    c_up = local(up_in, up)
    c_wg = local(wg_in, wg_raw)
    c_wu = local(wu_in, wu_raw)
    c_li = local(li_in, inputs.at[core, :, own])

    barrier = pltpu.get_barrier_semaphore()
    partners = [X_UP, X_DN, X_OP, Y_UP, Y_DN, Y_OP, H_UP, H_DN, SIB] + L_TO
    for where in partners:
        pl.semaphore_signal(barrier, inc=1, device_id=where, device_id_type=MESH)
    pl.semaphore_wait(barrier, len(partners))

    def g(block):
        return grads.at[core, :, block]

    def gt(t, block):
        return grads.at[core, t, block]

    TO_H = ((ho, H_OP), (hm, H_UP), (hp, H_DN))
    TO_Y = (Y_OP, Y_UP, Y_DN)
    g_z = [[arrival() for _ in range(3)] for _ in range(PARTS)]
    g_own = arrival()
    for t, k in ((0, 1), (1, 2)):
        send(og_in.at[t], gt(t, own), TO_H[k][1], OUT_A, g_z[t][k])
    for where in TO_Y:
        send(og_in, g(own), where, OUT_A, g_own)

    def padded(raw, ref, copy):
        copy.wait()
        ref[core, 0:units, :] = raw[...]
        ref[core, units:WIDE, :] = jnp.zeros((WIDE - units, feats), BF)
        arrived = arrival()
        same(ref.at[core], SIB, OUT_W, arrived)
        return arrived

    s_wd = padded(wd_raw, wd, c_wd)
    c_gp.wait()
    c_up.wait()
    pre[core] = jnp.zeros((2, 2, 32, WIDE), BF)
    for half in (0, 1):
        pre[core, half, 0, :, 0:units] = gp[half * 32 : half * 32 + 32, :]
        pre[core, half, 1, :, 0:units] = up[half * 32 : half * 32 + 32, :]
    s_pre = arrival()
    same(pre.at[core, sib], SIB, OUT_H, s_pre)
    for half in (0, 1):
        gate = pre[core, half, 0].astype(F32)
        value = rounded(gate * jax.nn.sigmoid(gate) * pre[core, half, 1].astype(F32))
        hidden[half, :, row] = value.reshape(PARTS, RT, WIDE)

    def h(block):
        return hidden.at[:, :, block]

    h_x, h_z = arrival(), arrival()
    h_one = [arrival() for _ in range(4)]
    for where in (X_OP, X_UP, X_DN):
        same(h(row), where, OUT_H, h_x)

    g_y = [arrival() for _ in range(PARTS)]
    def g_from_z(t, k):
        block = gt(t, at(y, TO_H[k][0]))
        wait(g_z[t][k], block)
        if (t, k) in ((0, 1), (1, 2)):
            same(block, TO_H[k][1], OUT_A, g_z[t][0])
            send(og_in.at[1 - t], gt(1 - t, own), TO_H[k][1], OUT_A, g_z[1 - t][k])
        for where in TO_Y:
            same(block, where, OUT_A, g_y[t])

    for t, k in ((0, 1), (1, 2), (0, 2), (1, 1), (0, 0), (1, 0)):
        g_from_z(t, k)

    def li(block):
        return inputs.at[core, :, block]

    i_z = arrival()
    for _, where in TO_H:
        send(li_in, li(own), where, OUT_A, i_z)

    def on_core(k, what, *args):
        @pl.when(core == k)
        def _():
            what(*args)

    def hidden_z():
        for where in L_TO:
            same(h(row), where, OUT_H, h_z)

    def hidden_x():
        wait(h_z, hidden.at[:, :, pl.ds(0, 3)])
        one, two, three = [h(at(x, on(zl, -d))) for d in (1, 2, 3)]
        same(two, X_UP, OUT_H, h_one[0])
        same(one, X_DN, OUT_H, h_one[2])
        same(three, X_UP, OUT_H, h_one[1])
        same(three, X_DN, OUT_H, h_one[3])
        same(one, X_UP, OUT_H, h_x)
        same(two, X_DN, OUT_H, h_x)

    def hidden_forward():
        ref = h(at(xm, on(zl, -2)))
        wait(h_one[0], ref)
        same(ref, X_UP, OUT_H, h_x)
        ref = h(at(xp, on(zl, -1)))
        wait(h_one[2], ref)
        same(ref, X_DN, OUT_H, h_x)
        wait(h_one[1], ref)
        same(hidden.at[0, :, at(xm, on(zl, -3))], X_UP, OUT_H, h_x)
        wait(h_one[3], ref)
        same(hidden.at[1, :, at(xp, on(zl, -3))], X_DN, OUT_H, h_x)

    on_core(1, hidden_z)

    def partial(t, j):
        rows = grads[core, t].reshape(16 * RT, feats)
        out = dot(rows, wd[j], NT).reshape(16, RT, WIDE)
        part[t * 2 + j] = out
        part_bf[t * 2 + j] = rounded(out)

    n_units = 2 * PARTS
    x_in = [arrival() for _ in range(n_units)]
    z_in = [arrival() for _ in range(n_units)]

    def begin(u):
        for k, (a, where) in enumerate(((xo, X_OP), (xp, X_UP), (xm, X_DN))):
            send(part_bf.at[u, pl.ds(a * 4, 4)], x_recv.at[u, k], where, OUT_B, x_in[u])

    def x_sum(u, b):
        out = part[u, at(x, b)]
        for k in range(3):
            out = out + x_recv[u, k, b].astype(F32)
        return out

    def along_z(u):
        wait(x_in[u], x_recv.at[u])
        for d in (2, 1, 3):
            z_send[u, d - 1] = rounded(x_sum(u, on(zl, d)))
            send(z_send.at[u, d - 1], z_recv.at[u, d - 1], L_TO[d - 1], OUT_B, z_in[u])

    c_og.wait()
    wait(s_wd, wd.at[sib])
    wait(g_own, grads.at[0, :, pl.ds(0, 3)])
    wait(g_y[0], grads.at[0, 0, pl.ds(0, 9)])
    partial(0, 0)
    begin(0)
    partial(0, 1)
    begin(1)
    wait(g_y[1], grads.at[0, 0, pl.ds(0, 9)])
    partial(1, 0)
    begin(2)
    partial(1, 1)
    begin(3)
    along_z(0)
    along_z(1)
    s_g = arrival()
    same(grads.at[core], SIB, OUT_W, s_g)
    s_wg = padded(wg_raw, wg, c_wg)
    s_wu = padded(wu_raw, wu, c_wu)
    along_z(2)

    along_z(3)
    on_core(1, hidden_x)
    wait(s_pre, pre.at[sib, core])

    def b_ref(t, a, b):
        return backs.at[t, at(a, b)]

    b_z = [[arrival() for _ in range(3)] for _ in range(PARTS)]
    b_one = [[arrival() for _ in range(4)] for _ in range(PARTS)]
    b_up = [arrival() for _ in range(PARTS)]
    b_dn = [arrival() for _ in range(PARTS)]
    b_far = [arrival() for _ in range(PARTS)]
    b_opp = [arrival() for _ in range(PARTS)]

    def start_backs(t):
        for j in (0, 1):
            u = t * 2 + j
            wait(z_in[u], z_recv.at[u])
            back = x_sum(u, zl)
            for d in (1, 2, 3):
                back = back + z_recv[u, d - 1].astype(F32)
            rows = pl.ds(t * RT, RT)
            gate = pre[j, core, 0, rows].astype(F32)
            upper = pre[j, core, 1, rows].astype(F32)
            sig = jax.nn.sigmoid(gate)
            backs[t, row, 0, j] = rounded(back * upper * sig * (1.0 + gate * (1.0 - sig)))
            backs[t, row, 1, j] = rounded(back * gate * sig)
        for d in (2, 1, 3):
            same(backs.at[t, row], L_TO[d - 1], OUT_C, b_z[t][d - 1])
        on_core(0, same, backs.at[t, row], X_OP, OUT_C, b_opp[t])
        on_core(1, same, backs.at[t, row], X_OP, OUT_C, b_far[t])
        same(backs.at[t, row], X_UP, OUT_C, b_up[t])
        same(backs.at[t, row], X_DN, OUT_C, b_dn[t])

    start_backs(0)

    wait(i_z, inputs.at[0, :, pl.ds(0, 3)])
    c_li.wait()
    i_y = arrival()
    for where in TO_Y:
        same(inputs.at[core, :, pl.ds(y * 4, 4)], where, OUT_H, i_y)
    start_backs(1)

    def from_z(t, d):
        ref = b_ref(t, x, on(zl, -d))
        wait(b_z[t][d - 1], ref)
        if d != 1:
            same(ref, X_UP, OUT_C, b_one[t][0 if d == 2 else 1])
        if d != 2:
            same(ref, X_DN, OUT_C, b_one[t][2 if d == 1 else 3])

    def opposite_to_z(t):
        ref = b_ref(t, xo, zl)
        wait(b_opp[t], ref)
        for d in (2, 1, 3):
            same(ref, L_TO[d - 1], OUT_C, b_far[t])

    def from_z_last(t, d):
        ref = b_ref(t, x, on(zl, -d))
        wait(b_z[t][d - 1], ref)
        same(ref, X_UP, OUT_C, b_up[t])
        same(ref, X_DN, OUT_C, b_dn[t])

    def last_x(t):
        same(b_ref(t, x, on(zl, -1)), X_UP, OUT_C, b_up[t])
        same(b_ref(t, x, on(zl, -2)), X_DN, OUT_C, b_dn[t])

    def forward(t, d):
        up_ref, dn_ref = b_ref(t, xm, on(zl, -d)), b_ref(t, xp, on(zl, -d))
        if d == 2:
            wait(b_one[t][0], up_ref)
            same(up_ref, X_UP, OUT_C, b_far[t])
        elif d == 1:
            wait(b_one[t][2], dn_ref)
            same(dn_ref, X_DN, OUT_C, b_far[t])
        else:
            wait(b_one[t][1], up_ref)
            same(up_ref.at[0], X_UP, OUT_C, b_far[t])
            wait(b_one[t][3], dn_ref)
            same(dn_ref.at[1], X_DN, OUT_C, b_far[t])

    s_b = arrival()
    q_y = [arrival() for _ in range(PARTS)]
    q_z = [arrival() for _ in range(PARTS)]

    def to_y(t, a):
        @pl.when(a != y)
        def _():
            where = (row, at(a, zh) * 2 + core)
            send(iq_bf.at[t, pl.ds(a * 4, 4)], i_recv.at[t, y], where, OUT_D, q_y[t])

    def use(t, planes):
        total = None
        for k, weight in ((0, wg), (1, wu)):
            for j in (0, 1):
                rows = [backs[t, pl.ds(a * 4, 4), k, j].reshape(4 * RT, WIDE) for a in planes]
                rows = rows[0] if len(rows) == 1 else jnp.concatenate(rows, axis=0)
                term = dot(rows, weight[j], NN)
                total = term if total is None else total + term
        for k, a in enumerate(planes):
            out = total[k * 4 * RT : (k + 1) * 4 * RT].reshape(4, RT, feats)
            some = pl.ds(a * 4, 4)
            iq[t, some] = out
            iq_bf[t, some] = rounded(out)
            to_y(t, a)
            send(backs.at[t, some, :, sib], backs_sib.at[t, some], SIB, OUT_S, s_b)

    def y_sum(t, b):
        out = iq[t, at(y, b)]
        for k in range(3):
            out = out + i_recv[t, on(y, k + 1), b].astype(F32)
        return out

    def along_h(t):
        wait(q_y[t], i_recv.at[t, pl.ds(0, 3)])
        for k, (b, where) in enumerate(((ho, H_OP), (hp, H_UP), (hm, H_DN))):
            iz_send[t, k] = rounded(y_sum(t, b))
            send(iz_send.at[t, k], iz_recv.at[t, k], where, OUT_D, q_z[t])

    def finish(t):
        wait(q_z[t], iz_recv.at[t])
        total = y_sum(t, zh)
        for k in range(3):
            total = total + iz_recv[t, k].astype(F32)
        ig[t] = rounded(total)

    def gather_0():
        for t in range(PARTS):
            opposite_to_z(t)
            for d in (2, 1, 3):
                from_z_last(t, d)
        hidden_z()

    def gather_1():
        for d in (2, 1, 3):
            from_z(0, d)
        last_x(0)
        hidden_forward()
        forward(0, 2)
        forward(0, 1)
        for d in (2, 1, 3):
            from_z(1, d)
        forward(0, 3)
        last_x(1)
        forward(1, 2)

    on_core(0, gather_0)
    on_core(1, gather_1)

    def near_planes(t):
        for k, blocks in ((0, 4), (1, 2)):
            on_core(k, wait, b_up[t], backs.at[t, pl.ds(0, blocks)])
            on_core(k, wait, b_dn[t], backs.at[t, pl.ds(0, blocks)])

    def far_plane(t):
        for k, blocks in ((0, 3), (1, 4)):
            on_core(k, wait, b_far[t], backs.at[t, pl.ds(0, blocks)])

    wait(s_wg, wg.at[sib])
    wait(s_wu, wu.at[sib])
    near_planes(0)
    use(0, (x, xm, xp))
    on_core(1, forward, 1, 1)
    on_core(1, forward, 1, 3)
    far_plane(0)
    use(0, (xo,))
    wait(i_y, inputs.at[0, :, pl.ds(0, 12)])
    s_i = arrival()
    same(inputs.at[core], SIB, OUT_H, s_i)

    near_planes(1)
    use(1, (x, xm, xp))

    far_plane(1)
    use(1, (xo,))
    along_h(0)
    on_core(0, hidden_x)
    along_h(1)

    def tokens(value):
        return value.reshape(512, value.shape[-1])

    wait(s_i, inputs.at[sib])
    wait(s_b, backs_sib)
    on_core(0, hidden_forward)
    outs = []
    for k, ref, out in ((0, gg, gg_out), (1, ug, ug_out)):
        value = dot(tokens(backs[:, :, k, core]), tokens(inputs[core]), TN)
        value = value + dot(tokens(backs_sib[:, :, k]), tokens(inputs[sib]), TN)
        ref[...] = rounded(value[0:units, :])
        outs.append(local(ref, out))
    finish(0)
    wait(h_x, hidden.at[0])
    wait(s_g, grads.at[sib])
    dg[...] = rounded(
        dot(hidden[...].reshape(1024, WIDE), grads[...].reshape(1024, feats), TN)[0:units, :]
    )
    outs.append(local(dg, dg_out))
    finish(1)
    outs.append(local(ig, ig_out))

    wait_sent(OUT_A, grads.at[:, :, pl.ds(0, 9)])
    wait_sent(OUT_W, backs)
    wait_sent(OUT_H, backs.at[:, pl.ds(0, 15)])
    wait_sent(OUT_B, grads.at[:, :, pl.ds(0, 15)])
    wait_sent(OUT_C, backs.at[:, pl.ds(0, 15)])
    wait_sent(OUT_S, backs.at[0])
    wait_sent(OUT_D, grads.at[0, :, pl.ds(0, 15)])
    for copy in outs:
        copy.wait()
    assert len(arrivals) == N_ARRIVALS, len(arrivals)


def hand_over(*refs):
    sources, targets, rooms, sem = refs[:4], refs[4:8], refs[8:12], refs[12]
    into = [pltpu.make_async_copy(s, v, sem.at[k]) for k, (s, v) in enumerate(zip(sources, rooms))]
    out = [pltpu.make_async_copy(v, t, sem.at[4 + k]) for k, (v, t) in enumerate(zip(rooms, targets))]
    for copy in into:
        copy.start()
    for first, second in zip(into, out):
        first.wait()
        second.start()
    for copy in out:
        copy.wait()


def shards(out_grad, layer_input, gate_preact, up_preact, w_down, w_gate, w_up):
    tokens, feats = out_grad.shape
    units = gate_preact.shape[1]
    vm = pltpu.VMEM
    any_space = pl.BlockSpec(memory_space=pl.ANY)
    shapes = (
        jax.ShapeDtypeStruct((PARTS, RT, feats), BF),
        jax.ShapeDtypeStruct((units, feats), BF),
        jax.ShapeDtypeStruct((units, feats), BF),
        jax.ShapeDtypeStruct((units, feats), BF),
    )
    results = pl.pallas_call(
        kernel,
        out_shape=shapes,
        in_specs=[any_space] * 7,
        out_specs=(any_space,) * 4,
        scratch_shapes=[
            vm((2, PARTS, 16, RT, feats), BF),
            vm((2, PARTS, 16, RT, feats), BF),
            vm((2, PARTS, 16, RT, WIDE), BF),
            vm((PARTS, 16, 2, 2, RT, WIDE), BF),
            vm((PARTS, 16, 2, RT, WIDE), BF),
            vm((64, units), BF), vm((64, units), BF), vm((2, 2, 2, 32, WIDE), BF),
            vm((units, feats), BF), vm((units, feats), BF), vm((units, feats), BF),
            vm((2, WIDE, feats), BF), vm((2, WIDE, feats), BF), vm((2, WIDE, feats), BF),
            vm((2 * PARTS, 16, RT, WIDE), F32), vm((2 * PARTS, 16, RT, WIDE), BF),
            vm((2 * PARTS, 3, 4, RT, WIDE), BF),
            vm((2 * PARTS, 3, RT, WIDE), BF), vm((2 * PARTS, 3, RT, WIDE), BF),
            vm((PARTS, 16, RT, feats), F32), vm((PARTS, 16, RT, feats), BF),
            vm((PARTS, 4, 4, RT, feats), BF),
            vm((PARTS, 3, RT, feats), BF), vm((PARTS, 3, RT, feats), BF),
            vm((units, feats), BF), vm((units, feats), BF), vm((units, feats), BF),
            vm((PARTS, RT, feats), BF),
            pltpu.SemaphoreType.DMA((11,)),
            pltpu.SemaphoreType.DMA((N_GROUPS,)),
            pltpu.SemaphoreType.DMA((N_ARRIVALS,)),
        ],
        compiler_params=pltpu.CompilerParams(
            collective_id=0, has_side_effects=True, vmem_limit_bytes=VMEM_ALL
        ),
        cost_estimate=pl.CostEstimate(
            flops=12 * 1024 * units * feats, bytes_accessed=3_000_000, transcendentals=64 * units
        ),
        name="swiglu_back",
    )(
        out_grad.reshape(PARTS, RT, feats),
        layer_input.reshape(PARTS, RT, feats),
        gate_preact,
        up_preact,
        w_down.T,
        w_gate,
        w_up,
    )
    ig, dg, gg, ug = pl.pallas_call(
        hand_over,
        out_shape=shapes,
        in_specs=[any_space] * 4,
        out_specs=(any_space,) * 4,
        scratch_shapes=[vm(s.shape, s.dtype) for s in shapes] + [pltpu.SemaphoreType.DMA((8,))],
        compiler_params=pltpu.CompilerParams(vmem_limit_bytes=VMEM_ALL),
        name="hand_over",
    )(*results)
    return ig.reshape(tokens, feats), dg.T, gg, ug


def solution(mesh):
    return jax.shard_map(
        shards,
        mesh=mesh,
        in_specs=(
            P("col", "row"),
            P("col", "row"),
            P("row", "col"),
            P("row", "col"),
            P("row", "col"),
            P("col", "row"),
            P("col", "row"),
        ),
        out_specs=(P("col", "row"), P("row", "col"), P("col", "row"), P("col", "row")),
        check_vma=False,
    )
```

```python
import jax
import jax.numpy as jnp
from jax import lax
from jax.experimental import pallas as pl
from jax.experimental.pallas import tpu as pltpu
from jax.sharding import PartitionSpec as P

BF = jnp.bfloat16
F32 = jnp.float32
MESH = pl.DeviceIdType.MESH
N_GROUPS = 7
N_ARRIVALS = 58
WIDE = 512
PARTS = 2
RT = 32 // PARTS
VMEM_ALL = 64 * 1024 * 1024 - 65536


def rounded(value):
    return value.astype(BF)


def dot(left, right, dims):
    return lax.dot_general(left, right, (dims, ((), ())), preferred_element_type=F32)


NN = ((1,), (0,))
NT = ((1,), (1,))
TN = ((0,), (0,))


def kernel(
    og_in, li_in, gp_in, up_in, wd_in, wg_in, wu_in,
    ig_out, dg_out, gg_out, ug_out,
    grads, inputs, hidden, backs, backs_sib,
    gp, up, pre, wd_raw, wg_raw, wu_raw, wd, wg, wu,
    part, part_bf, x_recv, z_send, z_recv,
    iq, iq_bf, i_recv, iz_send, iz_recv,
    gg, ug, dg, ig,
    local_sem, send_sem, recv_sem,
):
    units = gp_in.shape[1]
    feats = og_in.shape[2]
    row, col = lax.axis_index("row"), lax.axis_index("col")
    x, zl = lax.div(row, 4), lax.rem(row, 4)
    y, zh, core = lax.div(col, 8), lax.rem(lax.div(col, 2), 4), lax.rem(col, 2)
    sib = 1 - core

    def on(value, step):
        return lax.rem(value + step + 4, 4)

    xp, xm, xo = on(x, 1), on(x, -1), on(x, 2)
    yp, ym, yo = on(y, 1), on(y, -1), on(y, 2)
    hp, hm, ho = on(zh, 1), on(zh, -1), on(zh, 2)

    def at(a, b):
        return a * 4 + b

    X_UP, X_DN, X_OP = [(at(a, zl), col) for a in (xp, xm, xo)]
    Y_UP, Y_DN, Y_OP = [(row, at(a, zh) * 2 + core) for a in (yp, ym, yo)]
    H_UP, H_DN, H_OP = [(row, at(y, b) * 2 + core) for b in (hp, hm, ho)]
    L_TO = [(at(x, on(zl, d)), col) for d in (1, 2, 3)]
    SIB = (row, at(y, zh) * 2 + sib)

    locals_ = []

    def local(src, dst):
        copy = pltpu.make_async_copy(src, dst, local_sem.at[len(locals_)])
        locals_.append(copy)
        copy.start()
        return copy

    arrivals = []

    def arrival():
        arrivals.append(recv_sem.at[len(arrivals)])
        return arrivals[-1]

    def remote(src, dst, where, group, arrived):
        return pltpu.make_async_remote_copy(
            src_ref=src,
            dst_ref=dst,
            send_sem=send_sem.at[group],
            recv_sem=arrived,
            device_id=where,
            device_id_type=MESH,
        )

    def send(src, dst, where, group, arrived):
        remote(src, dst, where, group, arrived).start()

    def same(ref, where, group, arrived):
        remote(ref, ref, where, group, arrived).start()

    def wait(arrived, like):
        remote(like, like, SIB, 0, arrived).wait_recv()

    def wait_sent(group, like):
        remote(like, like, SIB, group, arrivals[0]).wait_send()

    OUT_A, OUT_W, OUT_H, OUT_B, OUT_C, OUT_S, OUT_D = range(N_GROUPS)

    own = at(y, zh)
    c_og = local(og_in, grads.at[core, :, own])
    c_wd = local(wd_in, wd_raw)
    c_gp = local(gp_in, gp)
    c_up = local(up_in, up)
    c_wg = local(wg_in, wg_raw)
    c_wu = local(wu_in, wu_raw)
    c_li = local(li_in, inputs.at[core, :, own])

    barrier = pltpu.get_barrier_semaphore()
    partners = [X_UP, X_DN, X_OP, Y_UP, Y_DN, Y_OP, H_UP, H_DN, SIB] + L_TO
    for where in partners:
        pl.semaphore_signal(barrier, inc=1, device_id=where, device_id_type=MESH)
    pl.semaphore_wait(barrier, len(partners))

    def g(block):
        return grads.at[core, :, block]

    def gt(t, block):
        return grads.at[core, t, block]

    TO_H = ((ho, H_OP), (hm, H_UP), (hp, H_DN))
    TO_Y = (Y_OP, Y_UP, Y_DN)
    g_z = [[arrival() for _ in range(3)] for _ in range(PARTS)]
    g_own = arrival()
    for t, k in ((0, 1), (1, 2)):
        send(og_in.at[t], gt(t, own), TO_H[k][1], OUT_A, g_z[t][k])
    for where in TO_Y:
        send(og_in, g(own), where, OUT_A, g_own)

    def padded(raw, ref, copy):
        copy.wait()
        ref[core, 0:units, :] = raw[...]
        ref[core, units:WIDE, :] = jnp.zeros((WIDE - units, feats), BF)
        arrived = arrival()
        same(ref.at[core], SIB, OUT_W, arrived)
        return arrived

    s_wd = padded(wd_raw, wd, c_wd)
    c_gp.wait()
    c_up.wait()
    pre[core] = jnp.zeros((2, 2, 32, WIDE), BF)
    for half in (0, 1):
        pre[core, half, 0, :, 0:units] = gp[half * 32 : half * 32 + 32, :]
        pre[core, half, 1, :, 0:units] = up[half * 32 : half * 32 + 32, :]
    s_pre = arrival()
    same(pre.at[core, sib], SIB, OUT_H, s_pre)
    for half in (0, 1):
        gate = pre[core, half, 0].astype(F32)
        value = rounded(gate * jax.nn.sigmoid(gate) * pre[core, half, 1].astype(F32))
        hidden[half, :, row] = value.reshape(PARTS, RT, WIDE)

    def h(block):
        return hidden.at[:, :, block]

    h_x, h_z = arrival(), arrival()
    h_one = [arrival() for _ in range(4)]
    for where in (X_OP, X_UP, X_DN):
        same(h(row), where, OUT_H, h_x)

    g_y = [arrival() for _ in range(PARTS)]
    def g_from_z(t, k):
        block = gt(t, at(y, TO_H[k][0]))
        wait(g_z[t][k], block)
        if (t, k) in ((0, 1), (1, 2)):
            same(block, TO_H[k][1], OUT_A, g_z[t][0])
            send(og_in.at[1 - t], gt(1 - t, own), TO_H[k][1], OUT_A, g_z[1 - t][k])
        for where in TO_Y:
            same(block, where, OUT_A, g_y[t])

    for t, k in ((0, 1), (1, 2), (0, 2), (1, 1), (0, 0), (1, 0)):
        g_from_z(t, k)

    def li(block):
        return inputs.at[core, :, block]

    i_z = arrival()
    for _, where in TO_H:
        send(li_in, li(own), where, OUT_A, i_z)

    def on_core(k, what, *args):
        @pl.when(core == k)
        def _():
            what(*args)

    def hidden_z():
        for where in L_TO:
            same(h(row), where, OUT_H, h_z)

    def hidden_x():
        wait(h_z, hidden.at[:, :, pl.ds(0, 3)])
        one, two, three = [h(at(x, on(zl, -d))) for d in (1, 2, 3)]
        same(two, X_UP, OUT_H, h_one[0])
        same(one, X_DN, OUT_H, h_one[2])
        same(three, X_UP, OUT_H, h_one[1])
        same(three, X_DN, OUT_H, h_one[3])
        same(one, X_UP, OUT_H, h_x)
        same(two, X_DN, OUT_H, h_x)

    def hidden_forward():
        ref = h(at(xm, on(zl, -2)))
        wait(h_one[0], ref)
        same(ref, X_UP, OUT_H, h_x)
        ref = h(at(xp, on(zl, -1)))
        wait(h_one[2], ref)
        same(ref, X_DN, OUT_H, h_x)
        wait(h_one[1], ref)
        same(hidden.at[0, :, at(xm, on(zl, -3))], X_UP, OUT_H, h_x)
        wait(h_one[3], ref)
        same(hidden.at[1, :, at(xp, on(zl, -3))], X_DN, OUT_H, h_x)

    on_core(1, hidden_z)

    def partial(t, j):
        rows = grads[core, t].reshape(16 * RT, feats)
        out = dot(rows, wd[j], NT).reshape(16, RT, WIDE)
        part[t * 2 + j] = out
        part_bf[t * 2 + j] = rounded(out)

    n_units = 2 * PARTS
    x_in = [arrival() for _ in range(n_units)]
    z_in = [arrival() for _ in range(n_units)]

    def begin(u):
        for k, (a, where) in enumerate(((xo, X_OP), (xp, X_UP), (xm, X_DN))):
            send(part_bf.at[u, pl.ds(a * 4, 4)], x_recv.at[u, k], where, OUT_B, x_in[u])

    def x_sum(u, b):
        out = part[u, at(x, b)]
        for k in range(3):
            out = out + x_recv[u, k, b].astype(F32)
        return out

    def along_z(u):
        wait(x_in[u], x_recv.at[u])
        for d in (2, 1, 3):
            z_send[u, d - 1] = rounded(x_sum(u, on(zl, d)))
            send(z_send.at[u, d - 1], z_recv.at[u, d - 1], L_TO[d - 1], OUT_B, z_in[u])

    c_og.wait()
    wait(s_wd, wd.at[sib])
    wait(g_own, grads.at[0, :, pl.ds(0, 3)])
    wait(g_y[0], grads.at[0, 0, pl.ds(0, 9)])
    partial(0, 0)
    begin(0)
    partial(0, 1)
    begin(1)
    wait(g_y[1], grads.at[0, 0, pl.ds(0, 9)])
    partial(1, 0)
    begin(2)
    partial(1, 1)
    begin(3)
    along_z(0)
    along_z(1)
    s_g = arrival()
    same(grads.at[core], SIB, OUT_W, s_g)
    s_wg = padded(wg_raw, wg, c_wg)
    s_wu = padded(wu_raw, wu, c_wu)
    along_z(2)

    along_z(3)
    on_core(1, hidden_x)
    wait(s_pre, pre.at[sib, core])

    def b_ref(t, a, b):
        return backs.at[t, at(a, b)]

    b_z = [[arrival() for _ in range(3)] for _ in range(PARTS)]
    b_one = [[arrival() for _ in range(4)] for _ in range(PARTS)]
    b_up = [arrival() for _ in range(PARTS)]
    b_dn = [arrival() for _ in range(PARTS)]
    b_far = [arrival() for _ in range(PARTS)]
    b_opp = [arrival() for _ in range(PARTS)]

    def over_three(d):
        return zl == {1: 3, 2: 4, 3: 0}[d]

    def pass_on(t, ref):
        pl.when(zl == 2)(lambda: same(ref, L_TO[0], OUT_C, b_z[t][2]))
        pl.when(zl == 1)(lambda: same(ref, L_TO[2], OUT_C, b_z[t][0]))

    def start_backs(t):
        for j in (0, 1):
            u = t * 2 + j
            wait(z_in[u], z_recv.at[u])
            back = x_sum(u, zl)
            for d in (1, 2, 3):
                back = back + z_recv[u, d - 1].astype(F32)
            rows = pl.ds(t * RT, RT)
            gate = pre[j, core, 0, rows].astype(F32)
            upper = pre[j, core, 1, rows].astype(F32)
            sig = jax.nn.sigmoid(gate)
            backs[t, row, 0, j] = rounded(back * upper * sig * (1.0 + gate * (1.0 - sig)))
            backs[t, row, 1, j] = rounded(back * gate * sig)
        for d in (2, 1, 3):
            pl.when(jnp.logical_not(over_three(d)))(
                lambda d=d: same(backs.at[t, row], L_TO[d - 1], OUT_C, b_z[t][d - 1])
            )
        on_core(0, same, backs.at[t, row], X_OP, OUT_C, b_opp[t])
        on_core(1, same, backs.at[t, row], X_OP, OUT_C, b_far[t])
        same(backs.at[t, row], X_UP, OUT_C, b_up[t])
        same(backs.at[t, row], X_DN, OUT_C, b_dn[t])

    start_backs(0)

    wait(i_z, inputs.at[0, :, pl.ds(0, 3)])
    c_li.wait()
    i_y = arrival()
    for where in TO_Y:
        same(inputs.at[core, :, pl.ds(y * 4, 4)], where, OUT_H, i_y)
    start_backs(1)

    def from_z(t, d):
        ref = b_ref(t, x, on(zl, -d))
        wait(b_z[t][d - 1], ref)
        if d == 2:
            pass_on(t, ref)
        if d != 1:
            same(ref, X_UP, OUT_C, b_one[t][0 if d == 2 else 1])
        if d != 2:
            same(ref, X_DN, OUT_C, b_one[t][2 if d == 1 else 3])

    def opposite_to_z(t):
        ref = b_ref(t, xo, zl)
        wait(b_opp[t], ref)
        for d in (2, 1, 3):
            same(ref, L_TO[d - 1], OUT_C, b_far[t])

    def from_z_last(t, d):
        ref = b_ref(t, x, on(zl, -d))
        wait(b_z[t][d - 1], ref)
        if d == 2:
            pass_on(t, ref)
        same(ref, X_UP, OUT_C, b_up[t])
        same(ref, X_DN, OUT_C, b_dn[t])

    def last_x(t):
        same(b_ref(t, x, on(zl, -1)), X_UP, OUT_C, b_up[t])
        same(b_ref(t, x, on(zl, -2)), X_DN, OUT_C, b_dn[t])

    def forward(t, d):
        up_ref, dn_ref = b_ref(t, xm, on(zl, -d)), b_ref(t, xp, on(zl, -d))
        if d == 2:
            wait(b_one[t][0], up_ref)
            same(up_ref, X_UP, OUT_C, b_far[t])
        elif d == 1:
            wait(b_one[t][2], dn_ref)
            same(dn_ref, X_DN, OUT_C, b_far[t])
        else:
            wait(b_one[t][1], up_ref)
            same(up_ref.at[0], X_UP, OUT_C, b_far[t])
            wait(b_one[t][3], dn_ref)
            same(dn_ref.at[1], X_DN, OUT_C, b_far[t])

    s_b = arrival()
    q_y = [arrival() for _ in range(PARTS)]
    q_z = [arrival() for _ in range(PARTS)]

    def to_y(t, a):
        @pl.when(a != y)
        def _():
            where = (row, at(a, zh) * 2 + core)
            send(iq_bf.at[t, pl.ds(a * 4, 4)], i_recv.at[t, y], where, OUT_D, q_y[t])

    def use(t, planes):
        total = None
        for k, weight in ((0, wg), (1, wu)):
            for j in (0, 1):
                rows = [backs[t, pl.ds(a * 4, 4), k, j].reshape(4 * RT, WIDE) for a in planes]
                rows = rows[0] if len(rows) == 1 else jnp.concatenate(rows, axis=0)
                term = dot(rows, weight[j], NN)
                total = term if total is None else total + term
        for k, a in enumerate(planes):
            out = total[k * 4 * RT : (k + 1) * 4 * RT].reshape(4, RT, feats)
            some = pl.ds(a * 4, 4)
            iq[t, some] = out
            iq_bf[t, some] = rounded(out)
            to_y(t, a)
            send(backs.at[t, some, :, sib], backs_sib.at[t, some], SIB, OUT_S, s_b)

    def y_sum(t, b):
        out = iq[t, at(y, b)]
        for k in range(3):
            out = out + i_recv[t, on(y, k + 1), b].astype(F32)
        return out

    def along_h(t):
        wait(q_y[t], i_recv.at[t, pl.ds(0, 3)])
        for k, (b, where) in enumerate(((ho, H_OP), (hp, H_UP), (hm, H_DN))):
            iz_send[t, k] = rounded(y_sum(t, b))
            send(iz_send.at[t, k], iz_recv.at[t, k], where, OUT_D, q_z[t])

    def finish(t):
        wait(q_z[t], iz_recv.at[t])
        total = y_sum(t, zh)
        for k in range(3):
            total = total + iz_recv[t, k].astype(F32)
        ig[t] = rounded(total)

    def gather_0():
        for t in range(PARTS):
            opposite_to_z(t)
            for d in (2, 1, 3):
                from_z_last(t, d)
        hidden_z()

    def gather_1():
        for d in (2, 1, 3):
            from_z(0, d)
        last_x(0)
        hidden_forward()
        forward(0, 2)
        forward(0, 1)
        for d in (2, 1, 3):
            from_z(1, d)
        forward(0, 3)
        last_x(1)
        forward(1, 2)

    on_core(0, gather_0)
    on_core(1, gather_1)

    def far_plane(t):
        for k, blocks in ((0, 3), (1, 4)):
            on_core(k, wait, b_far[t], backs.at[t, pl.ds(0, blocks)])

    wait(s_wg, wg.at[sib])
    wait(s_wu, wu.at[sib])
    def chunk_0(t):
        far_plane(t)
        use(t, (x, xo))
        wait(b_up[t], backs.at[t, pl.ds(0, 4)])
        use(t, (xm,))
        wait(b_dn[t], backs.at[t, pl.ds(0, 4)])
        use(t, (xp,))

    def chunk_1(t):
        wait(b_up[t], backs.at[t, pl.ds(0, 2)])
        wait(b_dn[t], backs.at[t, pl.ds(0, 2)])
        use(t, (x, xm, xp))
        if t == 0:
            forward(1, 1)
            forward(1, 3)
        far_plane(t)
        use(t, (xo,))

    on_core(0, chunk_0, 0)
    on_core(1, chunk_1, 0)
    wait(i_y, inputs.at[0, :, pl.ds(0, 12)])
    s_i = arrival()
    same(inputs.at[core], SIB, OUT_H, s_i)
    on_core(0, chunk_0, 1)
    on_core(1, chunk_1, 1)
    along_h(0)
    on_core(0, hidden_x)
    along_h(1)

    def tokens(value):
        return value.reshape(512, value.shape[-1])

    wait(s_i, inputs.at[sib])
    wait(s_b, backs_sib)
    on_core(0, hidden_forward)
    outs = []
    for k, ref, out in ((0, gg, gg_out), (1, ug, ug_out)):
        value = dot(tokens(backs[:, :, k, core]), tokens(inputs[core]), TN)
        value = value + dot(tokens(backs_sib[:, :, k]), tokens(inputs[sib]), TN)
        ref[...] = rounded(value[0:units, :])
        outs.append(local(ref, out))
    finish(0)
    wait(h_x, hidden.at[0])
    wait(s_g, grads.at[sib])
    dg[...] = rounded(
        dot(hidden[...].reshape(1024, WIDE), grads[...].reshape(1024, feats), TN)[0:units, :]
    )
    outs.append(local(dg, dg_out))
    finish(1)
    outs.append(local(ig, ig_out))

    wait_sent(OUT_A, grads.at[:, :, pl.ds(0, 9)])
    wait_sent(OUT_W, backs)
    wait_sent(OUT_H, backs.at[:, pl.ds(0, 15)])
    wait_sent(OUT_B, grads.at[:, :, pl.ds(0, 15)])
    ends = jnp.logical_or(zl == 0, zl == 3)
    pl.when(ends)(lambda: wait_sent(OUT_C, backs.at[:, pl.ds(0, 14)]))
    pl.when(jnp.logical_not(ends))(lambda: wait_sent(OUT_C, backs))
    wait_sent(OUT_S, backs.at[0])
    wait_sent(OUT_D, grads.at[0, :, pl.ds(0, 15)])
    for copy in outs:
        copy.wait()
    assert len(arrivals) == N_ARRIVALS, len(arrivals)


def hand_over(*refs):
    sources, targets, rooms, sem = refs[:4], refs[4:8], refs[8:12], refs[12]
    into = [pltpu.make_async_copy(s, v, sem.at[k]) for k, (s, v) in enumerate(zip(sources, rooms))]
    out = [pltpu.make_async_copy(v, t, sem.at[4 + k]) for k, (v, t) in enumerate(zip(rooms, targets))]
    for copy in into:
        copy.start()
    for first, second in zip(into, out):
        first.wait()
        second.start()
    for copy in out:
        copy.wait()


def shards(out_grad, layer_input, gate_preact, up_preact, w_down, w_gate, w_up):
    tokens, feats = out_grad.shape
    units = gate_preact.shape[1]
    vm = pltpu.VMEM
    any_space = pl.BlockSpec(memory_space=pl.ANY)
    shapes = (
        jax.ShapeDtypeStruct((PARTS, RT, feats), BF),
        jax.ShapeDtypeStruct((units, feats), BF),
        jax.ShapeDtypeStruct((units, feats), BF),
        jax.ShapeDtypeStruct((units, feats), BF),
    )
    results = pl.pallas_call(
        kernel,
        out_shape=shapes,
        in_specs=[any_space] * 7,
        out_specs=(any_space,) * 4,
        scratch_shapes=[
            vm((2, PARTS, 16, RT, feats), BF),
            vm((2, PARTS, 16, RT, feats), BF),
            vm((2, PARTS, 16, RT, WIDE), BF),
            vm((PARTS, 16, 2, 2, RT, WIDE), BF),
            vm((PARTS, 16, 2, RT, WIDE), BF),
            vm((64, units), BF), vm((64, units), BF), vm((2, 2, 2, 32, WIDE), BF),
            vm((units, feats), BF), vm((units, feats), BF), vm((units, feats), BF),
            vm((2, WIDE, feats), BF), vm((2, WIDE, feats), BF), vm((2, WIDE, feats), BF),
            vm((2 * PARTS, 16, RT, WIDE), F32), vm((2 * PARTS, 16, RT, WIDE), BF),
            vm((2 * PARTS, 3, 4, RT, WIDE), BF),
            vm((2 * PARTS, 3, RT, WIDE), BF), vm((2 * PARTS, 3, RT, WIDE), BF),
            vm((PARTS, 16, RT, feats), F32), vm((PARTS, 16, RT, feats), BF),
            vm((PARTS, 4, 4, RT, feats), BF),
            vm((PARTS, 3, RT, feats), BF), vm((PARTS, 3, RT, feats), BF),
            vm((units, feats), BF), vm((units, feats), BF), vm((units, feats), BF),
            vm((PARTS, RT, feats), BF),
            pltpu.SemaphoreType.DMA((11,)),
            pltpu.SemaphoreType.DMA((N_GROUPS,)),
            pltpu.SemaphoreType.DMA((N_ARRIVALS,)),
        ],
        compiler_params=pltpu.CompilerParams(
            collective_id=0, has_side_effects=True, vmem_limit_bytes=VMEM_ALL
        ),
        cost_estimate=pl.CostEstimate(
            flops=12 * 1024 * units * feats, bytes_accessed=3_000_000, transcendentals=64 * units
        ),
        name="swiglu_back",
    )(
        out_grad.reshape(PARTS, RT, feats),
        layer_input.reshape(PARTS, RT, feats),
        gate_preact,
        up_preact,
        w_down.T,
        w_gate,
        w_up,
    )
    ig, dg, gg, ug = pl.pallas_call(
        hand_over,
        out_shape=shapes,
        in_specs=[any_space] * 4,
        out_specs=(any_space,) * 4,
        scratch_shapes=[vm(s.shape, s.dtype) for s in shapes] + [pltpu.SemaphoreType.DMA((8,))],
        compiler_params=pltpu.CompilerParams(vmem_limit_bytes=VMEM_ALL),
        name="hand_over",
    )(*results)
    return ig.reshape(tokens, feats), dg.T, gg, ug


def solution(mesh):
    return jax.shard_map(
        shards,
        mesh=mesh,
        in_specs=(
            P("col", "row"),
            P("col", "row"),
            P("row", "col"),
            P("row", "col"),
            P("row", "col"),
            P("col", "row"),
            P("col", "row"),
        ),
        out_specs=(P("col", "row"), P("row", "col"), P("col", "row"), P("col", "row")),
        check_vma=False,
    )
```

```python
import jax
import jax.numpy as jnp
from jax import lax
from jax.experimental import pallas as pl
from jax.experimental.pallas import tpu as pltpu
from jax.sharding import PartitionSpec as P

BF = jnp.bfloat16
F32 = jnp.float32
MESH = pl.DeviceIdType.MESH
N_GROUPS = 7
N_ARRIVALS = 58
WIDE = 512
PARTS = 2
RT = 32 // PARTS
VMEM_ALL = 64 * 1024 * 1024 - 65536


def rounded(value):
    return value.astype(BF)


def dot(left, right, dims):
    return lax.dot_general(left, right, (dims, ((), ())), preferred_element_type=F32)


NN = ((1,), (0,))
NT = ((1,), (1,))
TN = ((0,), (0,))


def kernel(
    og_in, li_in, gp_in, up_in, wd_in, wg_in, wu_in,
    ig_out, dg_out, gg_out, ug_out,
    grads, inputs, hidden, backs, backs_sib,
    gp, up, pre, wd_raw, wg_raw, wu_raw, wd, wg, wu,
    part, part_bf, x_recv, z_send, z_recv,
    iq, iq_bf, i_recv, iz_send, iz_recv,
    gg, ug, dg, ig,
    local_sem, send_sem, recv_sem,
):
    units = gp_in.shape[1]
    feats = og_in.shape[2]
    row, col = lax.axis_index("row"), lax.axis_index("col")
    x, zl = lax.div(row, 4), lax.rem(row, 4)
    y, zh, core = lax.div(col, 8), lax.rem(lax.div(col, 2), 4), lax.rem(col, 2)
    sib = 1 - core

    def on(value, step):
        return lax.rem(value + step + 4, 4)

    xp, xm, xo = on(x, 1), on(x, -1), on(x, 2)
    yp, ym, yo = on(y, 1), on(y, -1), on(y, 2)
    hp, hm, ho = on(zh, 1), on(zh, -1), on(zh, 2)

    def at(a, b):
        return a * 4 + b

    X_UP, X_DN, X_OP = [(at(a, zl), col) for a in (xp, xm, xo)]
    Y_UP, Y_DN, Y_OP = [(row, at(a, zh) * 2 + core) for a in (yp, ym, yo)]
    H_UP, H_DN, H_OP = [(row, at(y, b) * 2 + core) for b in (hp, hm, ho)]
    L_TO = [(at(x, on(zl, d)), col) for d in (1, 2, 3)]
    SIB = (row, at(y, zh) * 2 + sib)

    barrier = pltpu.get_barrier_semaphore()
    partners = [H_UP, H_DN] + L_TO + [X_OP, Y_OP, X_UP, X_DN, Y_UP, Y_DN, SIB]
    for where in partners:
        pl.semaphore_signal(barrier, inc=1, device_id=where, device_id_type=MESH)

    locals_ = []

    def local(src, dst):
        copy = pltpu.make_async_copy(src, dst, local_sem.at[len(locals_)])
        locals_.append(copy)
        copy.start()
        return copy

    arrivals = []

    def arrival():
        arrivals.append(recv_sem.at[len(arrivals)])
        return arrivals[-1]

    def remote(src, dst, where, group, arrived):
        return pltpu.make_async_remote_copy(
            src_ref=src,
            dst_ref=dst,
            send_sem=send_sem.at[group],
            recv_sem=arrived,
            device_id=where,
            device_id_type=MESH,
        )

    def send(src, dst, where, group, arrived):
        remote(src, dst, where, group, arrived).start()

    def same(ref, where, group, arrived):
        remote(ref, ref, where, group, arrived).start()

    def wait(arrived, like):
        remote(like, like, SIB, 0, arrived).wait_recv()

    def wait_sent(group, like):
        remote(like, like, SIB, group, arrivals[0]).wait_send()

    OUT_A, OUT_W, OUT_H, OUT_B, OUT_C, OUT_S, OUT_D = range(N_GROUPS)

    own = at(y, zh)
    c_og = local(og_in, grads.at[core, :, own])
    c_wd = local(wd_in, wd_raw)
    c_gp = local(gp_in, gp)
    c_up = local(up_in, up)
    c_wg = local(wg_in, wg_raw)
    c_wu = local(wu_in, wu_raw)
    c_li = local(li_in, inputs.at[core, :, own])

    pl.semaphore_wait(barrier, len(partners))

    def g(block):
        return grads.at[core, :, block]

    def gt(t, block):
        return grads.at[core, t, block]

    TO_H = ((ho, H_OP), (hm, H_UP), (hp, H_DN))
    TO_Y = (Y_OP, Y_UP, Y_DN)
    g_z = [[arrival() for _ in range(3)] for _ in range(PARTS)]
    g_own = arrival()
    for t, k in ((0, 1), (1, 2)):
        send(og_in.at[t], gt(t, own), TO_H[k][1], OUT_A, g_z[t][k])
    for where in TO_Y:
        send(og_in, g(own), where, OUT_A, g_own)

    def padded(raw, ref, copy):
        copy.wait()
        ref[core, 0:units, :] = raw[...]
        ref[core, units:WIDE, :] = jnp.zeros((WIDE - units, feats), BF)
        arrived = arrival()
        same(ref.at[core], SIB, OUT_W, arrived)
        return arrived

    s_wd = padded(wd_raw, wd, c_wd)
    c_gp.wait()
    c_up.wait()
    pre[core] = jnp.zeros((2, 2, 32, WIDE), BF)
    for half in (0, 1):
        pre[core, half, 0, :, 0:units] = gp[half * 32 : half * 32 + 32, :]
        pre[core, half, 1, :, 0:units] = up[half * 32 : half * 32 + 32, :]
    s_pre = arrival()
    same(pre.at[core, sib], SIB, OUT_H, s_pre)
    for half in (0, 1):
        gate = pre[core, half, 0].astype(F32)
        value = rounded(gate * jax.nn.sigmoid(gate) * pre[core, half, 1].astype(F32))
        hidden[half, :, row] = value.reshape(PARTS, RT, WIDE)

    def h(block):
        return hidden.at[:, :, block]

    h_x, h_z = arrival(), arrival()
    h_one = [arrival() for _ in range(4)]
    for where in (X_OP, X_UP, X_DN):
        same(h(row), where, OUT_H, h_x)

    g_y = [arrival() for _ in range(PARTS)]
    def g_from_z(t, k):
        block = gt(t, at(y, TO_H[k][0]))
        wait(g_z[t][k], block)
        if (t, k) in ((0, 1), (1, 2)):
            same(block, TO_H[k][1], OUT_A, g_z[t][0])
            send(og_in.at[1 - t], gt(1 - t, own), TO_H[k][1], OUT_A, g_z[1 - t][k])
        for where in TO_Y:
            same(block, where, OUT_A, g_y[t])

    for t, k in ((0, 1), (1, 2), (0, 2), (1, 1), (0, 0), (1, 0)):
        g_from_z(t, k)

    def li(block):
        return inputs.at[core, :, block]

    i_z = arrival()
    for _, where in TO_H:
        send(li_in, li(own), where, OUT_A, i_z)

    def on_core(k, what, *args):
        @pl.when(core == k)
        def _():
            what(*args)

    def hidden_z():
        for where in L_TO:
            same(h(row), where, OUT_H, h_z)

    def hidden_x():
        wait(h_z, hidden.at[:, :, pl.ds(0, 3)])
        one, two, three = [h(at(x, on(zl, -d))) for d in (1, 2, 3)]
        same(two, X_UP, OUT_H, h_one[0])
        same(one, X_DN, OUT_H, h_one[2])
        same(three, X_UP, OUT_H, h_one[1])
        same(three, X_DN, OUT_H, h_one[3])
        same(one, X_UP, OUT_H, h_x)
        same(two, X_DN, OUT_H, h_x)

    def hidden_forward():
        ref = h(at(xm, on(zl, -2)))
        wait(h_one[0], ref)
        same(ref, X_UP, OUT_H, h_x)
        ref = h(at(xp, on(zl, -1)))
        wait(h_one[2], ref)
        same(ref, X_DN, OUT_H, h_x)
        wait(h_one[1], ref)
        same(hidden.at[0, :, at(xm, on(zl, -3))], X_UP, OUT_H, h_x)
        wait(h_one[3], ref)
        same(hidden.at[1, :, at(xp, on(zl, -3))], X_DN, OUT_H, h_x)

    on_core(1, hidden_z)

    def partial(t, j):
        rows = grads[core, t].reshape(16 * RT, feats)
        out = dot(rows, wd[j], NT).reshape(16, RT, WIDE)
        part[t * 2 + j] = out
        part_bf[t * 2 + j] = rounded(out)

    n_units = 2 * PARTS
    x_in = [arrival() for _ in range(n_units)]
    z_in = [arrival() for _ in range(n_units)]

    def begin(u):
        for k, (a, where) in enumerate(((xo, X_OP), (xp, X_UP), (xm, X_DN))):
            send(part_bf.at[u, pl.ds(a * 4, 4)], x_recv.at[u, k], where, OUT_B, x_in[u])

    def x_sum(u, b):
        out = part[u, at(x, b)]
        for k in range(3):
            out = out + x_recv[u, k, b].astype(F32)
        return out

    def along_z(u):
        wait(x_in[u], x_recv.at[u])
        for d in (2, 1, 3):
            z_send[u, d - 1] = rounded(x_sum(u, on(zl, d)))
            send(z_send.at[u, d - 1], z_recv.at[u, d - 1], L_TO[d - 1], OUT_B, z_in[u])

    c_og.wait()
    wait(s_wd, wd.at[sib])
    wait(g_own, grads.at[0, :, pl.ds(0, 3)])
    wait(g_y[0], grads.at[0, 0, pl.ds(0, 9)])
    partial(0, 0)
    begin(0)
    partial(0, 1)
    begin(1)
    wait(g_y[1], grads.at[0, 0, pl.ds(0, 9)])
    partial(1, 0)
    begin(2)
    partial(1, 1)
    begin(3)
    along_z(0)
    along_z(1)
    s_g = arrival()
    same(grads.at[core], SIB, OUT_W, s_g)
    s_wg = padded(wg_raw, wg, c_wg)
    s_wu = padded(wu_raw, wu, c_wu)
    along_z(2)

    along_z(3)
    on_core(1, hidden_x)
    wait(s_pre, pre.at[sib, core])

    def b_ref(t, a, b):
        return backs.at[t, at(a, b)]

    b_z = [[arrival() for _ in range(3)] for _ in range(PARTS)]
    b_one = [[arrival() for _ in range(4)] for _ in range(PARTS)]
    b_up = [arrival() for _ in range(PARTS)]
    b_dn = [arrival() for _ in range(PARTS)]
    b_far = [arrival() for _ in range(PARTS)]
    b_opp = [arrival() for _ in range(PARTS)]

    def over_three(d):
        return zl == {1: 3, 2: 4, 3: 0}[d]

    def pass_on(t, ref):
        pl.when(zl == 2)(lambda: same(ref, L_TO[0], OUT_C, b_z[t][2]))
        pl.when(zl == 1)(lambda: same(ref, L_TO[2], OUT_C, b_z[t][0]))

    def start_backs(t):
        for j in (0, 1):
            u = t * 2 + j
            wait(z_in[u], z_recv.at[u])
            back = x_sum(u, zl)
            for d in (1, 2, 3):
                back = back + z_recv[u, d - 1].astype(F32)
            rows = pl.ds(t * RT, RT)
            gate = pre[j, core, 0, rows].astype(F32)
            upper = pre[j, core, 1, rows].astype(F32)
            sig = jax.nn.sigmoid(gate)
            backs[t, row, 0, j] = rounded(back * upper * sig * (1.0 + gate * (1.0 - sig)))
            backs[t, row, 1, j] = rounded(back * gate * sig)
        for d in (2, 1, 3):
            pl.when(jnp.logical_not(over_three(d)))(
                lambda d=d: same(backs.at[t, row], L_TO[d - 1], OUT_C, b_z[t][d - 1])
            )
        on_core(0, same, backs.at[t, row], X_OP, OUT_C, b_opp[t])
        on_core(1, same, backs.at[t, row], X_OP, OUT_C, b_far[t])
        same(backs.at[t, row], X_UP, OUT_C, b_up[t])
        same(backs.at[t, row], X_DN, OUT_C, b_dn[t])

    start_backs(0)

    wait(i_z, inputs.at[0, :, pl.ds(0, 3)])
    c_li.wait()
    i_y = arrival()
    for where in TO_Y:
        same(inputs.at[core, :, pl.ds(y * 4, 4)], where, OUT_H, i_y)
    start_backs(1)

    def from_z(t, d):
        ref = b_ref(t, x, on(zl, -d))
        wait(b_z[t][d - 1], ref)
        if d == 2:
            pass_on(t, ref)
        if d != 1:
            same(ref, X_UP, OUT_C, b_one[t][0 if d == 2 else 1])
        if d != 2:
            same(ref, X_DN, OUT_C, b_one[t][2 if d == 1 else 3])

    def opposite_to_z(t):
        ref = b_ref(t, xo, zl)
        wait(b_opp[t], ref)
        for d in (2, 1, 3):
            same(ref, L_TO[d - 1], OUT_C, b_far[t])

    def from_z_last(t, d):
        ref = b_ref(t, x, on(zl, -d))
        wait(b_z[t][d - 1], ref)
        if d == 2:
            pass_on(t, ref)
        same(ref, X_UP, OUT_C, b_up[t])
        same(ref, X_DN, OUT_C, b_dn[t])

    def last_x(t):
        same(b_ref(t, x, on(zl, -1)), X_UP, OUT_C, b_up[t])
        same(b_ref(t, x, on(zl, -2)), X_DN, OUT_C, b_dn[t])

    def forward(t, d):
        up_ref, dn_ref = b_ref(t, xm, on(zl, -d)), b_ref(t, xp, on(zl, -d))
        if d == 2:
            wait(b_one[t][0], up_ref)
            same(up_ref, X_UP, OUT_C, b_far[t])
        elif d == 1:
            wait(b_one[t][2], dn_ref)
            same(dn_ref, X_DN, OUT_C, b_far[t])
        else:
            wait(b_one[t][1], up_ref)
            same(up_ref.at[0], X_UP, OUT_C, b_far[t])
            wait(b_one[t][3], dn_ref)
            same(dn_ref.at[1], X_DN, OUT_C, b_far[t])

    s_b = arrival()
    q_y = [arrival() for _ in range(PARTS)]
    q_z = [arrival() for _ in range(PARTS)]

    def to_y(t, a):
        @pl.when(a != y)
        def _():
            where = (row, at(a, zh) * 2 + core)
            send(iq_bf.at[t, pl.ds(a * 4, 4)], i_recv.at[t, y], where, OUT_D, q_y[t])

    def use(t, planes):
        total = None
        for k, weight in ((0, wg), (1, wu)):
            for j in (0, 1):
                rows = [backs[t, pl.ds(a * 4, 4), k, j].reshape(4 * RT, WIDE) for a in planes]
                rows = rows[0] if len(rows) == 1 else jnp.concatenate(rows, axis=0)
                term = dot(rows, weight[j], NN)
                total = term if total is None else total + term
        for k, a in enumerate(planes):
            out = total[k * 4 * RT : (k + 1) * 4 * RT].reshape(4, RT, feats)
            some = pl.ds(a * 4, 4)
            iq[t, some] = out
            iq_bf[t, some] = rounded(out)
            to_y(t, a)
            send(backs.at[t, some, :, sib], backs_sib.at[t, some], SIB, OUT_S, s_b)

    def y_sum(t, b):
        out = iq[t, at(y, b)]
        for k in range(3):
            out = out + i_recv[t, on(y, k + 1), b].astype(F32)
        return out

    def along_h(t):
        wait(q_y[t], i_recv.at[t, pl.ds(0, 3)])
        for k, (b, where) in enumerate(((ho, H_OP), (hp, H_UP), (hm, H_DN))):
            iz_send[t, k] = rounded(y_sum(t, b))
            send(iz_send.at[t, k], iz_recv.at[t, k], where, OUT_D, q_z[t])

    def finish(t):
        wait(q_z[t], iz_recv.at[t])
        total = y_sum(t, zh)
        for k in range(3):
            total = total + iz_recv[t, k].astype(F32)
        ig[t] = rounded(total)

    def gather_0():
        for t in range(PARTS):
            opposite_to_z(t)
            for d in (2, 1, 3):
                from_z_last(t, d)
        hidden_z()

    def gather_1():
        for d in (2, 1, 3):
            from_z(0, d)
        last_x(0)
        hidden_forward()
        forward(0, 2)
        forward(0, 1)
        for d in (2, 1, 3):
            from_z(1, d)
        forward(0, 3)
        last_x(1)
        forward(1, 2)
        forward(1, 1)
        forward(1, 3)

    on_core(0, gather_0)
    on_core(1, gather_1)

    def far_plane(t):
        for k, blocks in ((0, 3), (1, 4)):
            on_core(k, wait, b_far[t], backs.at[t, pl.ds(0, blocks)])

    wait(s_wg, wg.at[sib])
    wait(s_wu, wu.at[sib])
    def chunk_0(t):
        far_plane(t)
        use(t, (x, xo))
        wait(b_up[t], backs.at[t, pl.ds(0, 4)])
        use(t, (xm,))
        wait(b_dn[t], backs.at[t, pl.ds(0, 4)])
        use(t, (xp,))

    def chunk_1(t):
        wait(b_up[t], backs.at[t, pl.ds(0, 2)])
        wait(b_dn[t], backs.at[t, pl.ds(0, 2)])
        use(t, (x, xm, xp))
        far_plane(t)
        use(t, (xo,))

    on_core(0, chunk_0, 0)
    on_core(1, chunk_1, 0)
    wait(i_y, inputs.at[0, :, pl.ds(0, 12)])
    s_i = arrival()
    same(inputs.at[core], SIB, OUT_H, s_i)
    on_core(0, chunk_0, 1)
    on_core(1, chunk_1, 1)
    along_h(0)
    on_core(0, hidden_x)
    along_h(1)

    def tokens(value):
        return value.reshape(512, value.shape[-1])

    wait(s_i, inputs.at[sib])
    wait(s_b, backs_sib)
    on_core(0, hidden_forward)
    outs = []
    for k, ref, out in ((0, gg, gg_out), (1, ug, ug_out)):
        value = dot(tokens(backs[:, :, k, core]), tokens(inputs[core]), TN)
        value = value + dot(tokens(backs_sib[:, :, k]), tokens(inputs[sib]), TN)
        ref[...] = rounded(value[0:units, :])
        outs.append(local(ref, out))
    finish(0)
    wait(h_x, hidden.at[0])
    wait(s_g, grads.at[sib])
    dg[...] = rounded(
        dot(hidden[...].reshape(1024, WIDE), grads[...].reshape(1024, feats), TN)[0:units, :]
    )
    outs.append(local(dg, dg_out))
    finish(1)
    outs.append(local(ig, ig_out))

    wait_sent(OUT_A, grads.at[:, :, pl.ds(0, 9)])
    wait_sent(OUT_W, backs)
    wait_sent(OUT_H, backs.at[:, pl.ds(0, 15)])
    wait_sent(OUT_B, grads.at[:, :, pl.ds(0, 15)])
    ends = jnp.logical_or(zl == 0, zl == 3)
    pl.when(ends)(lambda: wait_sent(OUT_C, backs.at[:, pl.ds(0, 14)]))
    pl.when(jnp.logical_not(ends))(lambda: wait_sent(OUT_C, backs))
    wait_sent(OUT_S, backs.at[0])
    wait_sent(OUT_D, grads.at[0, :, pl.ds(0, 15)])
    for copy in outs:
        copy.wait()
    assert len(arrivals) == N_ARRIVALS, len(arrivals)


def hand_over(*refs):
    sources, targets, rooms, sem = refs[:4], refs[4:8], refs[8:12], refs[12]
    into = [pltpu.make_async_copy(s, v, sem.at[k]) for k, (s, v) in enumerate(zip(sources, rooms))]
    out = [pltpu.make_async_copy(v, t, sem.at[4 + k]) for k, (v, t) in enumerate(zip(rooms, targets))]
    for copy in into:
        copy.start()
    for first, second in zip(into, out):
        first.wait()
        second.start()
    for copy in out:
        copy.wait()


def shards(out_grad, layer_input, gate_preact, up_preact, w_down, w_gate, w_up):
    tokens, feats = out_grad.shape
    units = gate_preact.shape[1]
    vm = pltpu.VMEM
    any_space = pl.BlockSpec(memory_space=pl.ANY)
    shapes = (
        jax.ShapeDtypeStruct((PARTS, RT, feats), BF),
        jax.ShapeDtypeStruct((units, feats), BF),
        jax.ShapeDtypeStruct((units, feats), BF),
        jax.ShapeDtypeStruct((units, feats), BF),
    )
    results = pl.pallas_call(
        kernel,
        out_shape=shapes,
        in_specs=[any_space] * 7,
        out_specs=(any_space,) * 4,
        scratch_shapes=[
            vm((2, PARTS, 16, RT, feats), BF),
            vm((2, PARTS, 16, RT, feats), BF),
            vm((2, PARTS, 16, RT, WIDE), BF),
            vm((PARTS, 16, 2, 2, RT, WIDE), BF),
            vm((PARTS, 16, 2, RT, WIDE), BF),
            vm((64, units), BF), vm((64, units), BF), vm((2, 2, 2, 32, WIDE), BF),
            vm((units, feats), BF), vm((units, feats), BF), vm((units, feats), BF),
            vm((2, WIDE, feats), BF), vm((2, WIDE, feats), BF), vm((2, WIDE, feats), BF),
            vm((2 * PARTS, 16, RT, WIDE), F32), vm((2 * PARTS, 16, RT, WIDE), BF),
            vm((2 * PARTS, 3, 4, RT, WIDE), BF),
            vm((2 * PARTS, 3, RT, WIDE), BF), vm((2 * PARTS, 3, RT, WIDE), BF),
            vm((PARTS, 16, RT, feats), F32), vm((PARTS, 16, RT, feats), BF),
            vm((PARTS, 4, 4, RT, feats), BF),
            vm((PARTS, 3, RT, feats), BF), vm((PARTS, 3, RT, feats), BF),
            vm((units, feats), BF), vm((units, feats), BF), vm((units, feats), BF),
            vm((PARTS, RT, feats), BF),
            pltpu.SemaphoreType.DMA((11,)),
            pltpu.SemaphoreType.DMA((N_GROUPS,)),
            pltpu.SemaphoreType.DMA((N_ARRIVALS,)),
        ],
        compiler_params=pltpu.CompilerParams(
            collective_id=0, has_side_effects=True, vmem_limit_bytes=VMEM_ALL
        ),
        cost_estimate=pl.CostEstimate(
            flops=12 * 1024 * units * feats, bytes_accessed=3_000_000, transcendentals=64 * units
        ),
        name="swiglu_back",
    )(
        out_grad.reshape(PARTS, RT, feats),
        layer_input.reshape(PARTS, RT, feats),
        gate_preact,
        up_preact,
        w_down.T,
        w_gate,
        w_up,
    )
    ig, dg, gg, ug = pl.pallas_call(
        hand_over,
        out_shape=shapes,
        in_specs=[any_space] * 4,
        out_specs=(any_space,) * 4,
        scratch_shapes=[vm(s.shape, s.dtype) for s in shapes] + [pltpu.SemaphoreType.DMA((8,))],
        compiler_params=pltpu.CompilerParams(vmem_limit_bytes=VMEM_ALL),
        name="hand_over",
    )(*results)
    return ig.reshape(tokens, feats), dg.T, gg, ug


def solution(mesh):
    return jax.shard_map(
        shards,
        mesh=mesh,
        in_specs=(
            P("col", "row"),
            P("col", "row"),
            P("row", "col"),
            P("row", "col"),
            P("row", "col"),
            P("col", "row"),
            P("col", "row"),
        ),
        out_specs=(P("col", "row"), P("row", "col"), P("col", "row"), P("col", "row")),
        check_vma=False,
    )
```
